128 devices in a mesh: expert: 128 (over x, y, z, core).
Axes of the slice: x: 4, y: 4, z: 4, core: 2. Of those that a mesh axis runs over, the one named last changes fastest.
Arguments:
- tokens: bfloat16 [16384, 3584], P('expert'), may hold values from -6 to 6
- cotangent: bfloat16 [16384, 3584], P('expert'), may hold values from -6 to 6
- routes: int32 [16384, 8], P('expert'), may hold values from 0 to 63, all different within a row; in each aligned block of 128 rows (0 to 127, 128 to 255, ...) at most 20 rows name the same one
- gates: bfloat16 [16384, 8], P('expert'), may hold values from 0.049804688 to 0.29882812
- previous_row: int32 [64], replicated, may hold values from 0 to 63, each once
- gu_payload: bfloat16 [64, 3584, 2048], P(None, 'expert'), may hold values from -0.09375 to 0.09375
- gu_scales: float32 [64, 28, 16], replicated, may hold values from 0.5 to 2
- down_payload: bfloat16 [64, 1024, 3584], P(None, 'expert'), may hold values from -0.1875 to 0.1875
- down_scales: float32 [64, 8, 28], replicated, may hold values from 0.5 to 2
Outputs:
- layer_out: bfloat16 [16384, 3584], P('expert')
- gate_grad: float32 [16384, 8], P('expert')
The draws below stay inside these ranges and needn't reach their ends.
Inputs may be any that keep to these rules, and one draw needn't show every extreme that they name: `routes`: each token names 8 different experts; among the tokens of one device no expert is named by more than 20 of them, and in some devices' tokens one expert is named by exactly 20. `previous_row`: each stored row holds exactly one expert.
All inputs are finite; a program needn't handle non-finite values.
Results may differ from the reference program's by a relative error of at most 0.0076.
Values may be sent and summed in bfloat16 or wider, within the bound.
No kernel may reach another device: no remote copies, remote signals or barrier semaphores. Data moves between devices by JAX's collectives and lax.ppermute only.
A program may use at most 256 MiB of HBM per device.

```python
import math
import jax
import jax.numpy as jnp
import numpy as np
from jax import lax

D = 3584
FF = 1024
TOP = 8
TOK_DEV = 128
SLOTS = 128
EXPERTS = 64
MOST = 20
TOKENS = 16384


def steps_of(key, shape, cuts, smallest, largest):
    level, own = 1.0, jax.random.fold_in(key, 6)
    for axis_at, blocks in cuts:
        heights = jnp.exp(jax.random.uniform(jax.random.fold_in(own, axis_at), (blocks,), jnp.float32, smallest / len(cuts), largest / len(cuts)))
        level = level * jnp.repeat(heights, shape[axis_at] // blocks).reshape([-1 if axis == axis_at else 1 for axis in range(len(shape))])
    return level


def deal_out(own_key, own, number, rows, amount, top, limit, skew):
    sequence = jax.random.permutation(own_key, amount)
    heavy_load, ordinary = shares(amount, rows * top, limit, skew, True), shares(amount, rows * top, limit, skew, False)
    places = jnp.arange(amount)

    def named(lengths, rotation):
        used = int((lengths > 0).sum())
        fixed = max(1, used // 4)
        shifted = fixed + (places - fixed + rotation * (used - fixed)) % max(1, amount - fixed)
        return jnp.zeros((amount,), jnp.int32).at[sequence[jnp.where(places < fixed, places, shifted)]].set(jnp.asarray(lengths, jnp.int32))

    lengths = jnp.where(number % 4 == 0, named(heavy_load, number // 4), named(ordinary, number - number // 4 - 1))
    mixed = jax.random.permutation(jax.random.fold_in(own, 3), amount)
    source_of, sink = mixed[0:amount // 2 * 2:2], mixed[1:amount // 2 * 2:2]
    room = jnp.minimum(lengths[source_of] - 1, limit - lengths[sink]) // 2
    room = jnp.where((source_of == sequence[0]) | (sink == sequence[0]) | (lengths[sink] == 0), 0, jnp.maximum(room, 0))
    shifted = jax.random.randint(jax.random.fold_in(own, 4), (amount // 2,), 0, 1 << 20) % (room + 1)
    lengths = lengths.at[source_of].add(-shifted).at[sink].add(shifted)
    labels = jnp.searchsorted(jnp.cumsum(lengths), jnp.arange(rows * top), side="right").astype(jnp.int32)
    grid = labels.reshape(top, rows).T
    grid = grid[jax.random.permutation(jax.random.fold_in(own, 1), rows)]
    rotation = jax.random.randint(jax.random.fold_in(own, 2), (rows, 1), 0, top)
    return jnp.take_along_axis(grid, (jnp.arange(top)[None, :] + rotation) % top, axis=1)


def shares(amount, total, most, skew, full):
    weights = [(1 << 20) // math.isqrt(standing ** skew) + 1 for standing in range(1, amount + 1)]
    largest = most if full else min(most, max(-(-total // amount), total * weights[0] // sum(weights)))
    least = 1 if total - largest >= amount - 1 else 0
    holding, spare = [largest] + [least] * (amount - 1), total - largest - least * (amount - 1)
    while spare > 0:
        free = [i for i in range(1, amount) if holding[i] < largest] or [i for i in range(1, amount) if holding[i] < most]
        whole, left = sum([weights[i] for i in free]), spare
        for i in free:
            more = min(most - holding[i], max(1, left * weights[i] // whole), spare)
            holding[i] = holding[i] + more
            spare = spare - more
    return np.array(holding)


def normal_values(own_key, shape, spread, bound, cuts=(), held_as=jnp.bfloat16):
    values = spread * jax.random.normal(own_key, shape, jnp.float32)
    if cuts:
        values = values * steps_of(own_key, shape, cuts, -0.22, 0.18)
    return jnp.clip(values, -bound, bound).astype(held_as)


def setup_inputs(seed: int = 0) -> dict:
    seeds = jax.random.split(jax.random.key(seed), 10)
    tokens = normal_values(seeds[0], (TOKENS, D), 1.0, 6.0, ((0, 128),))
    cotangent = normal_values(seeds[1], (TOKENS, D), 1.0, 6.0, ((0, 128),))
    routes_keys = jax.random.split(jax.random.fold_in(seeds[2], 1), TOKENS // TOK_DEV)
    routes_turns = jax.random.permutation(jax.random.fold_in(seeds[2], 3), TOKENS // TOK_DEV)
    routes = jax.vmap(lambda own, number: deal_out(jax.random.fold_in(seeds[2], 2), own, number, TOK_DEV, EXPERTS, TOP, MOST, 2))(routes_keys, routes_turns).reshape((TOKENS, TOP))
    gates = jnp.clip(0.049804688 + 0.24902344 * jax.random.uniform(seeds[3], (TOKENS, TOP), jnp.float32) ** steps_of(seeds[3], (TOKENS, TOP), ((0, 128),), -0.2, 0.2), 0.049804688, 0.29882812).astype(jnp.bfloat16)
    previous_row = jax.random.permutation(seeds[4], EXPERTS).astype(jnp.int32)
    gu_payload = normal_values(seeds[5], (EXPERTS, D, 2 * FF), D ** -0.5, 0.09375, ((1, 128),))
    gu_scales = jnp.clip(jnp.exp(jax.random.uniform(seeds[6], (EXPERTS, D // 128, 2 * FF // 128), jnp.float32, math.log(0.5), math.log(2.0))), 0.5, 2.0)
    down_payload = normal_values(seeds[7], (EXPERTS, FF, D), FF ** -0.5, 0.1875, ((1, 128),))
    down_scales = jnp.clip(jnp.exp(jax.random.uniform(seeds[8], (EXPERTS, FF // 128, D // 128), jnp.float32, math.log(0.5), math.log(2.0))), 0.5, 2.0)
    return {"tokens": tokens, "cotangent": cotangent, "routes": routes, "gates": gates, "previous_row": previous_row, "gu_payload": gu_payload, "gu_scales": gu_scales, "down_payload": down_payload, "down_scales": down_scales}


def dequantize(payload, scales):
    expanded = jnp.repeat(jnp.repeat(scales, 128, axis=0), 128, axis=1)
    return (payload.astype(jnp.float32) * expanded).astype(jnp.bfloat16)


def reference(tokens, cotangent, routes, gates, previous_row, gu_payload, gu_scales, down_payload, down_scales):
    flat_routes = routes.reshape(-1)
    route_count = flat_routes.shape[0]
    row_limit = MOST * SLOTS
    token_of = jnp.arange(route_count, dtype=jnp.int32) // TOP
    route_ids = jnp.arange(route_count, dtype=jnp.int32)

    def one_expert(gathered, expert):
        is_match = (flat_routes == expert).astype(jnp.int32)
        route_rank = jnp.cumsum(is_match) - 1
        target = jnp.where(is_match == 1, route_rank, row_limit).astype(jnp.int32)
        token_table = jnp.zeros((row_limit,), jnp.int32).at[target].set(token_of, mode="drop")
        route_table = jnp.full((row_limit,), route_count, jnp.int32).at[target].set(route_ids, mode="drop")
        stored = previous_row[expert]
        w_gu = dequantize(gu_payload[stored], gu_scales[stored])
        w_down = dequantize(down_payload[stored], down_scales[stored])
        hidden = jnp.dot(tokens[token_table], w_gu, preferred_element_type=jnp.float32)
        active = (jax.nn.silu(hidden[:, :FF]) * hidden[:, FF:]).astype(jnp.bfloat16)
        result = jnp.dot(active, w_down, preferred_element_type=jnp.float32).astype(jnp.bfloat16)
        return gathered.at[route_table].set(result, mode="drop"), None

    start = jnp.zeros((route_count, D), jnp.bfloat16)
    per_route, unused = lax.scan(one_expert, start, jnp.arange(EXPERTS, dtype=jnp.int32))
    stacked = per_route.reshape(-1, TOP, D).astype(jnp.float32)
    layer_out = jnp.einsum("tk,tkd->td", gates.astype(jnp.float32), stacked).astype(jnp.bfloat16)
    gate_grad = jnp.einsum("td,tkd->tk", cotangent.astype(jnp.float32), stacked)
    return layer_out, gate_grad
```

```python
import jax
import jax.numpy as jnp
from jax import lax
from jax.experimental import pallas as pl
from jax.experimental.pallas import tpu as pltpu
from jax.sharding import PartitionSpec as P

FF = 1024
TOP = 8
MOST = 20
FIRST = 16


def gu_kernel(parity_ref, own_ref, other_ref, scale_ref, out_ref):
    step = pl.program_id(0)
    width = out_ref.shape[1]
    even_core = parity_ref[0] == 0
    parts = []
    for chip in range(own_ref.shape[0]):
        own = own_ref[chip].astype(jnp.float32)
        other = other_ref[chip].astype(jnp.float32)
        for rows in (jnp.where(even_core, own, other), jnp.where(even_core, other, own)):
            parts += [rows[:, g * width : (g + 1) * width] for g in range(3)]
            fold = rows[:, 3 * width :]
            parts.append(jnp.concatenate([fold[:4], fold[4:]], axis=1))
    values = jnp.concatenate(parts, axis=0)
    count = values.shape[0]
    low = (step * count) // 128
    high = jnp.minimum(low + 1, scale_ref.shape[0] - 1)
    row = step * count + lax.broadcasted_iota(jnp.int32, values.shape, 0)
    scale = jnp.where(row < 128 * (low + 1), scale_ref[pl.ds(low, 1), :], scale_ref[pl.ds(high, 1), :])
    out_ref[...] = (values * scale).astype(jnp.bfloat16)


def dequantize_gu(own, other, scales, parity):
    chips, _, packed = own.shape
    width = packed * 2 // 7
    return pl.pallas_call(
        gu_kernel,
        grid=(chips // 2,),
        in_specs=[
            pl.BlockSpec(memory_space=pltpu.SMEM),
            pl.BlockSpec((2, 8, packed), lambda i: (i, 0, 0)),
            pl.BlockSpec((2, 8, packed), lambda i: (i, 0, 0)),
            pl.BlockSpec(scales.shape, lambda i: (0, 0)),
        ],
        out_specs=pl.BlockSpec((112, width), lambda i: (i, 0)),
        out_shape=jax.ShapeDtypeStruct((chips * 56, width), jnp.bfloat16),
        compiler_params=pltpu.CompilerParams(vmem_limit_bytes=32 * 1024 * 1024),
        cost_estimate=pl.CostEstimate(flops=chips * 56 * width, bytes_accessed=chips * 56 * width * 4, transcendentals=0),
        name="dequantize_gu",
    )(parity, own, other, scales)


def down_kernel(parity_ref, own_ref, other_ref, scale_ref, out_ref):
    step = pl.program_id(0)
    even_core = parity_ref[0] == 0
    parts = []
    for chip in range(own_ref.shape[0]):
        own = own_ref[chip].astype(jnp.float32)
        other = other_ref[chip].astype(jnp.float32)
        parts += [jnp.where(even_core, own, other), jnp.where(even_core, other, own)]
    values = jnp.concatenate(parts, axis=0)
    scale = scale_ref[pl.ds(step * values.shape[0] // 128, 1), :]
    out_ref[...] = (values * scale).astype(jnp.bfloat16)


def dequantize_down(own, other, scales, parity):
    chips, _, width = own.shape
    return pl.pallas_call(
        down_kernel,
        grid=(chips // 4,),
        in_specs=[
            pl.BlockSpec(memory_space=pltpu.SMEM),
            pl.BlockSpec((4, 8, width), lambda i: (i, 0, 0)),
            pl.BlockSpec((4, 8, width), lambda i: (i, 0, 0)),
            pl.BlockSpec(scales.shape, lambda i: (0, 0)),
        ],
        out_specs=pl.BlockSpec((64, width), lambda i: (i, 0)),
        out_shape=jax.ShapeDtypeStruct((chips * 16, width), jnp.bfloat16),
        compiler_params=pltpu.CompilerParams(vmem_limit_bytes=32 * 1024 * 1024),
        cost_estimate=pl.CostEstimate(flops=chips * 16 * width, bytes_accessed=chips * 16 * width * 4, transcendentals=0),
        name="dequantize_down",
    )(parity, own, other, scales)


def shards(
    tokens, cotangent, routes, gates, previous_row, gu_payload, gu_scales, down_payload, down_scales
):
    local_count, model_width = tokens.shape
    devices = lax.axis_size("expert")
    experts = previous_row.shape[0]
    device_id = lax.axis_index("expert")
    chip, core = device_id // 2, device_id % 2
    parity = core.astype(jnp.int32).reshape(1)
    same_core = [[2 * c + p for c in range(experts)] for p in range(2)]
    swap = [(d, d ^ 1) for d in range(devices)]

    def exchange(x):
        return lax.all_to_all(x, "expert", 0, 0, axis_index_groups=same_core, tiled=True)

    down_own = exchange(down_payload)
    down_other = lax.ppermute(down_own, "expert", swap)

    packed_gu = jnp.concatenate(
        [gu_payload[:, 8 * g : 8 * g + 8] for g in range(3)]
        + [jnp.concatenate([gu_payload[:, 24:28, :FF], gu_payload[:, 24:28, FF:]], axis=1)],
        axis=2,
    )
    packed_gu, down_own = lax.optimization_barrier((packed_gu, down_own))
    gu_own = exchange(packed_gu)
    gu_other = lax.ppermute(gu_own, "expert", swap)

    routes_t = routes.T
    gates_t = gates.T.astype(jnp.float32)
    slots = jnp.arange(experts, dtype=jnp.int32)[None, :, None]
    target = jnp.sum(
        jnp.where(routes_t[:, None, :] == slots, previous_row[None, :, None], 0), axis=1
    )
    named = target[:, None, :] == slots
    member = jnp.any(named, axis=0)
    gate_of = jnp.sum(jnp.where(named, gates_t[:, None, :], 0.0), axis=0)
    earlier = jnp.arange(local_count)[:, None] < jnp.arange(local_count)[None, :]
    rank = jnp.dot(
        member.astype(jnp.bfloat16), earlier.astype(jnp.bfloat16), preferred_element_type=jnp.float32
    ).astype(jnp.int32)
    rank = jnp.where(member, rank, -1)

    w_down = dequantize_down(
        down_own, down_other, jnp.repeat(down_scales[chip], 128, axis=1), parity
    )
    w_gu = dequantize_gu(gu_own, gu_other, jnp.repeat(gu_scales[chip], 128, axis=1), parity)

    def chosen(start, count):
        places = jnp.arange(start, start + count, dtype=jnp.int32)[None, :, None]
        return rank[:, None, :] == places

    def dispatch(start, count, after):
        select = chosen(start, count).reshape(experts * count, local_count).astype(jnp.bfloat16)
        outgoing = jnp.dot(select, tokens, preferred_element_type=jnp.float32).astype(jnp.bfloat16)
        outgoing = outgoing.reshape(experts, count, model_width)
        outgoing, after = lax.optimization_barrier((outgoing, after))
        return exchange(outgoing), after

    def expert(arrived):
        rows = arrived.reshape(-1, model_width)
        hidden = jnp.dot(rows, w_gu, preferred_element_type=jnp.float32)
        active = (jax.nn.silu(hidden[:, :FF]) * hidden[:, FF:]).astype(jnp.bfloat16)
        result = jnp.dot(active, w_down, preferred_element_type=jnp.float32).astype(jnp.bfloat16)
        return result.reshape(arrived.shape)

    def combine(returned, start, count):
        mask = chosen(start, count)
        rows = returned.reshape(-1, model_width)
        weight = jnp.where(mask, gate_of[:, None, :], 0.0).astype(jnp.bfloat16)
        summed = lax.dot_general(
            weight.reshape(-1, local_count),
            rows,
            (((0,), (0,)), ((), ())),
            preferred_element_type=jnp.float32,
        )
        inner = lax.dot_general(
            rows, cotangent, (((1,), (1,)), ((), ())), preferred_element_type=jnp.float32
        ).reshape(mask.shape)
        return summed, jnp.sum(jnp.where(mask, inner, 0.0), axis=1)

    rest = MOST - FIRST
    arrived_a, gu_own = dispatch(0, FIRST, gu_own)
    arrived_b, arrived_a = dispatch(FIRST, rest, arrived_a)
    produced_a = expert(arrived_a)
    produced_a, arrived_b = lax.optimization_barrier((produced_a, arrived_b))
    returned_a = exchange(produced_a)
    produced_b = expert(arrived_b)
    produced_b, returned_a = lax.optimization_barrier((produced_b, returned_a))
    returned_b = exchange(produced_b)
    out_a, grad_a = combine(returned_a, 0, FIRST)
    out_b, grad_b = combine(returned_b, FIRST, rest)
    layer_out = (out_a + out_b).astype(jnp.bfloat16)
    grad = grad_a + grad_b
    gate_grad = jnp.sum(jnp.where(named, grad[None], 0.0), axis=1).T
    return (layer_out, gate_grad)


def solution(mesh):
    in_specs = (
        P("expert", None),
        P("expert", None),
        P("expert", None),
        P("expert", None),
        P(),
        P(None, "expert", None),
        P(),
        P(None, "expert", None),
        P(),
    )
    out_specs = (P("expert", None), P("expert", None))
    return jax.shard_map(shards, mesh=mesh, in_specs=in_specs, out_specs=out_specs, check_vma=False)
```

```python
import jax
import jax.numpy as jnp
from jax import lax
from jax.experimental import pallas as pl
from jax.experimental.pallas import tpu as pltpu
from jax.sharding import PartitionSpec as P

FF = 1024
TOP = 8
PEERS = 16
COLS = 256


def in_rows(block):
    return block.astype(jnp.float32).reshape(-1, block.shape[-1]).astype(jnp.bfloat16)


def gu_kernel(parity_ref, own_ref, other_ref, scale_ref, out_ref):
    step = pl.program_id(0)
    width = out_ref.shape[1]
    even_core = parity_ref[0] == 0
    parts = []
    for chip in range(own_ref.shape[0]):
        own = own_ref[chip].astype(jnp.float32)
        other = other_ref[chip].astype(jnp.float32)
        for rows in (jnp.where(even_core, own, other), jnp.where(even_core, other, own)):
            parts += [rows[:, g * width : (g + 1) * width] for g in range(3)]
            fold = rows[:, 3 * width :]
            parts.append(jnp.concatenate([fold[:4], fold[4:]], axis=1))
    values = jnp.concatenate(parts, axis=0)
    count = values.shape[0]
    low = (step * count) // 128
    high = jnp.minimum(low + 1, scale_ref.shape[0] - 1)
    row = step * count + lax.broadcasted_iota(jnp.int32, values.shape, 0)
    scale = jnp.where(row < 128 * (low + 1), scale_ref[pl.ds(low, 1), :], scale_ref[pl.ds(high, 1), :])
    out_ref[...] = (values * scale).astype(jnp.bfloat16)


def dequantize_gu(own, other, scales, parity):
    chips = own.shape[0]
    width = 2 * FF
    packed = width * 7 // 2
    return pl.pallas_call(
        gu_kernel,
        grid=(chips // 2,),
        in_specs=[
            pl.BlockSpec(memory_space=pltpu.SMEM),
            pl.BlockSpec((2, 8, packed), lambda i: (i, 0, 0)),
            pl.BlockSpec((2, 8, packed), lambda i: (i, 0, 0)),
            pl.BlockSpec(scales.shape, lambda i: (0, 0)),
        ],
        out_specs=pl.BlockSpec((112, width), lambda i: (i, 0)),
        out_shape=jax.ShapeDtypeStruct((chips * 56, width), jnp.bfloat16),
        compiler_params=pltpu.CompilerParams(vmem_limit_bytes=32 * 1024 * 1024),
        cost_estimate=pl.CostEstimate(flops=chips * 56 * width, bytes_accessed=chips * 56 * width * 4, transcendentals=0),
        name="dequantize_gu",
    )(parity, own, other, scales)


def down_kernel(parity_ref, own_ref, other_ref, scale_ref, out_ref):
    step = pl.program_id(0)
    even_core = parity_ref[0] == 0
    parts = []
    for chip in range(own_ref.shape[0]):
        own = own_ref[chip].astype(jnp.float32)
        other = other_ref[chip].astype(jnp.float32)
        parts += [jnp.where(even_core, own, other), jnp.where(even_core, other, own)]
    values = jnp.concatenate(parts, axis=0)
    scale = scale_ref[pl.ds(step * values.shape[0] // 128, 1), :]
    out_ref[...] = (values * scale).astype(jnp.bfloat16)


def dequantize_down(own, other, scales, parity):
    chips = own.shape[0]
    width = scales.shape[1]
    return pl.pallas_call(
        down_kernel,
        grid=(chips // 4,),
        in_specs=[
            pl.BlockSpec(memory_space=pltpu.SMEM),
            pl.BlockSpec((4, 8, width), lambda i: (i, 0, 2)),
            pl.BlockSpec((4, 8, width), lambda i: (i, 0, 2)),
            pl.BlockSpec(scales.shape, lambda i: (0, 0)),
        ],
        out_specs=pl.BlockSpec((64, width), lambda i: (i, 0)),
        out_shape=jax.ShapeDtypeStruct((chips * 16, width), jnp.bfloat16),
        compiler_params=pltpu.CompilerParams(vmem_limit_bytes=32 * 1024 * 1024),
        cost_estimate=pl.CostEstimate(flops=chips * 16 * width, bytes_accessed=chips * 16 * width * 4, transcendentals=0),
        name="dequantize_down",
    )(parity, own, other, scales)


def expert_kernel(x_ref, gu_hbm, down_hbm, out_ref, gu_ref, down_ref, rows_ref, active_ref, sems):
    step = pl.program_id(0)
    width = rows_ref.shape[1]
    half = width // 2
    eight = 8 * PEERS
    chunks = FF // COLS
    copies = []
    for j in range(chunks):
        for start in (j * COLS, FF + j * COLS):
            part = (slice(None), pl.ds(start, COLS))
            copies.append(
                pltpu.make_async_copy(gu_hbm.at[part], gu_ref.at[part], sems.at[len(copies)])
            )
    copies.append(pltpu.make_async_copy(down_hbm, down_ref, sems.at[len(copies)]))

    @pl.when(step == 0)
    def _():
        for copy in copies:
            copy.start()

    for q in range(0, PEERS, 4):
        for g in range(2):
            rows_ref[pl.ds(g * eight + 8 * q, 32), :] = in_rows(
                x_ref[q : q + 4, :, g * width : (g + 1) * width]
            )
        fold = [x_ref[p, :, 2 * width :].astype(jnp.float32) for p in range(q, q + 4)]
        for part, first in ((0, 0), (1, 4)):
            rows_ref[pl.ds(2 * eight + 4 * q, 16), pl.ds(part * half, half)] = jnp.concatenate(
                [f[first : first + 4] for f in fold], axis=0
            ).astype(jnp.bfloat16)

    for j in range(chunks):

        @pl.when(step == 0)
        def _():
            copies[2 * j].wait()
            copies[2 * j + 1].wait()

        gate = jnp.dot(
            rows_ref[...], gu_ref[:, j * COLS : (j + 1) * COLS], preferred_element_type=jnp.float32
        )
        up = jnp.dot(
            rows_ref[...],
            gu_ref[:, FF + j * COLS : FF + (j + 1) * COLS],
            preferred_element_type=jnp.float32,
        )
        active_ref[:, j * COLS : (j + 1) * COLS] = (gate / (1.0 + jnp.exp(-gate)) * up).astype(
            jnp.bfloat16
        )

    @pl.when(step == 0)
    def _():
        copies[-1].wait()

    for j in range(half // COLS):
        sides = []
        for side in range(2):
            at = side * half + j * COLS
            y = jnp.dot(
                active_ref[...], down_ref[:, at : at + COLS], preferred_element_type=jnp.float32
            )
            sides.append(y)
            for g in range(2):
                out_ref[:, :, g * width + at : g * width + at + COLS] = (
                    y[g * eight : (g + 1) * eight].reshape(PEERS, 8, COLS).astype(jnp.bfloat16)
                )
        for p in range(PEERS):
            at = 2 * eight + 4 * p
            out_ref[p, :, 2 * width + j * COLS : 2 * width + (j + 1) * COLS] = jnp.concatenate(
                [sides[0][at : at + 4], sides[1][at : at + 4]], axis=0
            ).astype(jnp.bfloat16)


def run_expert(arrived, w_gu, w_down):
    peers, _, packed = arrived.shape
    width = w_gu.shape[0]
    rows = peers * 20
    return pl.pallas_call(
        expert_kernel,
        grid=(peers // PEERS,),
        in_specs=[
            pl.BlockSpec((PEERS, 8, packed), lambda i: (i, 0, 0)),
            pl.BlockSpec(memory_space=pl.ANY),
            pl.BlockSpec(memory_space=pl.ANY),
        ],
        out_specs=pl.BlockSpec((PEERS, 8, packed), lambda i: (i, 0, 0)),
        out_shape=jax.ShapeDtypeStruct(arrived.shape, jnp.bfloat16),
        scratch_shapes=[
            pltpu.VMEM(w_gu.shape, jnp.bfloat16),
            pltpu.VMEM(w_down.shape, jnp.bfloat16),
            pltpu.VMEM((PEERS * 20, width), jnp.bfloat16),
            pltpu.VMEM((PEERS * 20, FF), jnp.bfloat16),
            pltpu.SemaphoreType.DMA((2 * FF // COLS + 1,)),
        ],
        compiler_params=pltpu.CompilerParams(vmem_limit_bytes=56 * 1024 * 1024),
        cost_estimate=pl.CostEstimate(
            flops=rows * width * FF * 6,
            bytes_accessed=rows * width * 4 + width * FF * 6,
            transcendentals=rows * FF,
        ),
        name="run_expert",
    )(arrived, w_gu, w_down)


def combine_kernel(x_ref, rank_ref, gate_ref, cotangent_ref, out_ref, grad_ref, sum_ref):
    step = pl.program_id(0)
    tokens, width = cotangent_ref.shape
    half = width // 2

    @pl.when(step == 0)
    def _():
        sum_ref[...] = jnp.zeros_like(sum_ref)

    rank = rank_ref[...][:, None, :]
    gate = gate_ref[...][:, None, :]
    shape = (PEERS, 8, tokens)
    row = lax.broadcasted_iota(jnp.int32, shape, 1)
    low = row < 4
    pieces = [
        (rank == row, 0, 0, width),
        (rank == row + 8, width, 0, width),
        ((rank == row + 16) & low, 2 * width, 0, half),
        ((rank == row + 12) & ~low, 2 * width, half, half),
    ]
    grad = jnp.zeros((PEERS, tokens), jnp.float32)
    for mask, source, place, count in pieces:
        rows = in_rows(x_ref[:, :, source : source + count])
        weight = jnp.where(mask, gate, 0.0).reshape(-1, tokens).astype(jnp.bfloat16)
        sum_ref[:, place : place + count] += lax.dot_general(
            weight, rows, (((0,), (0,)), ((), ())), preferred_element_type=jnp.float32
        )
        inner = lax.dot_general(
            rows,
            cotangent_ref[:, place : place + count],
            (((1,), (1,)), ((), ())),
            preferred_element_type=jnp.float32,
        )
        grad += jnp.sum(jnp.where(mask, inner.reshape(shape), 0.0), axis=1)
    grad_ref[...] = grad

    @pl.when(step == pl.num_programs(0) - 1)
    def _():
        out_ref[...] = sum_ref[...].astype(jnp.bfloat16)


def combine(returned, rank, gate_of, cotangent):
    peers, _, packed = returned.shape
    tokens, width = cotangent.shape
    return pl.pallas_call(
        combine_kernel,
        grid=(peers // PEERS,),
        in_specs=[
            pl.BlockSpec((PEERS, 8, packed), lambda i: (i, 0, 0)),
            pl.BlockSpec((PEERS, tokens), lambda i: (i, 0)),
            pl.BlockSpec((PEERS, tokens), lambda i: (i, 0)),
            pl.BlockSpec((tokens, width), lambda i: (0, 0)),
        ],
        out_specs=[
            pl.BlockSpec((tokens, width), lambda i: (0, 0)),
            pl.BlockSpec((PEERS, tokens), lambda i: (i, 0)),
        ],
        out_shape=[
            jax.ShapeDtypeStruct((tokens, width), jnp.bfloat16),
            jax.ShapeDtypeStruct((peers, tokens), jnp.float32),
        ],
        scratch_shapes=[pltpu.VMEM((tokens, width), jnp.float32)],
        compiler_params=pltpu.CompilerParams(vmem_limit_bytes=40 * 1024 * 1024),
        cost_estimate=pl.CostEstimate(
            flops=peers * 24 * tokens * width * 4,
            bytes_accessed=peers * 40 * width + tokens * width * 4,
            transcendentals=0,
        ),
        name="combine",
    )(returned, rank, gate_of, cotangent)


def shards(
    tokens, cotangent, routes, gates, previous_row, gu_payload, gu_scales, down_payload, down_scales
):
    local_count, model_width = tokens.shape
    half = model_width // 2
    devices = lax.axis_size("expert")
    experts = previous_row.shape[0]
    device_id = lax.axis_index("expert")
    chip, core = device_id // 2, device_id % 2
    parity = core.astype(jnp.int32).reshape(1)
    same_core = [[2 * c + p for c in range(experts)] for p in range(2)]
    swap = [(d, d ^ 1) for d in range(devices)]

    def exchange(x):
        return lax.all_to_all(x, "expert", 0, 0, axis_index_groups=same_core, tiled=True)

    packed = jnp.concatenate(
        [gu_payload[:, 8 * g : 8 * g + 8] for g in range(3)]
        + [jnp.concatenate([gu_payload[:, 24:28, :FF], gu_payload[:, 24:28, FF:]], axis=1)]
        + [down_payload],
        axis=2,
    )
    tokens, packed = lax.optimization_barrier((tokens, packed))
    own = exchange(packed)

    routes_t = routes.T
    gates_t = gates.T.astype(jnp.float32)
    slots = jnp.arange(experts, dtype=jnp.int32)[None, :, None]
    target = jnp.sum(
        jnp.where(routes_t[:, None, :] == slots, previous_row[None, :, None], 0), axis=1
    )
    named = target[:, None, :] == slots
    member = jnp.any(named, axis=0)
    gate_of = jnp.sum(jnp.where(named, gates_t[:, None, :], 0.0), axis=0)
    earlier = jnp.arange(local_count)[:, None] < jnp.arange(local_count)[None, :]
    rank = jnp.dot(
        member.astype(jnp.bfloat16), earlier.astype(jnp.bfloat16), preferred_element_type=jnp.float32
    ).astype(jnp.int32)
    rank = jnp.where(member, rank, -1)

    def picked(places):
        select = (rank[:, None, :] == places[None, :, None]).astype(jnp.bfloat16)
        rows = jnp.dot(
            select.reshape(-1, local_count), tokens, preferred_element_type=jnp.float32
        ).astype(jnp.bfloat16)
        return rows.reshape(experts, places.shape[0], model_width)

    eight = jnp.arange(8, dtype=jnp.int32)
    last = picked(16 + eight % 4)
    last = jnp.where(eight[None, :, None] < 4, last[:, :, :half], last[:, :, half:])
    outgoing = jnp.concatenate([picked(eight), picked(8 + eight), last], axis=2)

    outgoing, own = lax.optimization_barrier((outgoing, own))
    other = lax.ppermute(own, "expert", swap)
    arrived = exchange(outgoing)
    w_down = dequantize_down(own, other, jnp.repeat(down_scales[chip], 128, axis=1), parity)
    w_gu = dequantize_gu(own, other, jnp.repeat(gu_scales[chip], 128, axis=1), parity)
    w_gu, w_down, arrived = lax.optimization_barrier((w_gu, w_down, arrived))
    produced = run_expert(arrived, w_gu, w_down)
    returned = exchange(produced)
    layer_out, grad = combine(returned, rank, gate_of, cotangent)
    gate_grad = jnp.sum(jnp.where(named, grad[None], 0.0), axis=1).T
    return (layer_out, gate_grad)


def solution(mesh):
    in_specs = (
        P("expert", None),
        P("expert", None),
        P("expert", None),
        P("expert", None),
        P(),
        P(None, "expert", None),
        P(),
        P(None, "expert", None),
        P(),
    )
    out_specs = (P("expert", None), P("expert", None))
    return jax.shard_map(shards, mesh=mesh, in_specs=in_specs, out_specs=out_specs, check_vma=False)
```

```python
import functools

import jax
import jax.numpy as jnp
from jax import lax
from jax.experimental import pallas as pl
from jax.experimental.pallas import tpu as pltpu
from jax.sharding import PartitionSpec as P

FF = 1024
TOP = 8
COLS = 256
GROUP = 16


def in_rows(block):
    return block.astype(jnp.float32).reshape(-1, block.shape[-1]).astype(jnp.bfloat16)


def by_core(parity_ref, own_ref, other_ref, body):
    @pl.when(parity_ref[0] == 0)
    def _():
        body(own_ref, other_ref)

    @pl.when(parity_ref[0] != 0)
    def _():
        body(other_ref, own_ref)


def gu_kernel(parity_ref, own_ref, other_ref, scale_ref, out_ref):
    step = pl.program_id(0)
    width = out_ref.shape[1]

    def body(zero_ref, one_ref):
        tiles = []
        for chip in range(zero_ref.shape[0]):
            zero = [zero_ref[chip, :, g * width : (g + 1) * width] for g in range(3)]
            one = [one_ref[chip, :, g * width : (g + 1) * width] for g in range(3)]
            fold_zero = zero_ref[chip, :, 3 * width :].astype(jnp.float32)
            fold_one = one_ref[chip, :, 3 * width :].astype(jnp.float32)
            middle = jnp.concatenate(
                [
                    jnp.concatenate([fold_zero[:4], fold_one[:4]], axis=0),
                    jnp.concatenate([fold_zero[4:], fold_one[4:]], axis=0),
                ],
                axis=1,
            )
            tiles += zero + [middle] + one
        for pair in range(len(tiles) // 2):
            scaled = []
            for k in (2 * pair, 2 * pair + 1):
                at = (step * 8 * len(tiles) + 8 * k) // 128
                scaled.append(tiles[k].astype(jnp.float32) * scale_ref[pl.ds(at, 1), :])
            out_ref[16 * pair : 16 * pair + 16, :] = jnp.concatenate(scaled, axis=0).astype(
                jnp.bfloat16
            )

    by_core(parity_ref, own_ref, other_ref, body)


def dequantize_gu(own, other, scales, parity):
    chips, _, packed = own.shape
    width = 2 * FF
    return pl.pallas_call(
        gu_kernel,
        grid=(chips // 2,),
        in_specs=[
            pl.BlockSpec(memory_space=pltpu.SMEM),
            pl.BlockSpec((2, 8, packed), lambda i: (i, 0, 0)),
            pl.BlockSpec((2, 8, packed), lambda i: (i, 0, 0)),
            pl.BlockSpec(scales.shape, lambda i: (0, 0)),
        ],
        out_specs=pl.BlockSpec((112, width), lambda i: (i, 0)),
        out_shape=jax.ShapeDtypeStruct((chips * 56, width), jnp.bfloat16),
        compiler_params=pltpu.CompilerParams(vmem_limit_bytes=32 * 1024 * 1024),
        cost_estimate=pl.CostEstimate(
            flops=chips * 56 * width, bytes_accessed=chips * 56 * width * 4, transcendentals=0
        ),
        name="dequantize_gu",
    )(parity, own, other, scales)


def down_kernel(parity_ref, own_ref, other_ref, scale_ref, out_ref):
    step = pl.program_id(0)
    chips = own_ref.shape[0]
    scale = scale_ref[pl.ds(step * chips * 16 // 128, 1), :]

    def body(zero_ref, one_ref):
        for chip in range(chips):
            both = [ref[chip].astype(jnp.float32) * scale for ref in (zero_ref, one_ref)]
            out_ref[16 * chip : 16 * chip + 16, :] = jnp.concatenate(both, axis=0).astype(
                jnp.bfloat16
            )

    by_core(parity_ref, own_ref, other_ref, body)


def dequantize_down(own, other, scales, parity):
    chips, _, width = own.shape
    return pl.pallas_call(
        down_kernel,
        grid=(chips // 8,),
        in_specs=[
            pl.BlockSpec(memory_space=pltpu.SMEM),
            pl.BlockSpec((8, 8, width), lambda i: (i, 0, 0)),
            pl.BlockSpec((8, 8, width), lambda i: (i, 0, 0)),
            pl.BlockSpec(scales.shape, lambda i: (0, 0)),
        ],
        out_specs=pl.BlockSpec((128, width), lambda i: (i, 0)),
        out_shape=jax.ShapeDtypeStruct((chips * 16, width), jnp.bfloat16),
        compiler_params=pltpu.CompilerParams(vmem_limit_bytes=32 * 1024 * 1024),
        cost_estimate=pl.CostEstimate(
            flops=chips * 16 * width, bytes_accessed=chips * 16 * width * 4, transcendentals=0
        ),
        name="dequantize_down",
    )(parity, own, other, scales)


def expert_kernel(place, x_ref, gu_hbm, down_hbm, *refs):
    out_ref, gu_ref, down_ref, rows_ref, active_ref, sems = refs[-6:]
    step = pl.program_id(0)
    peers, _, packed = x_ref.shape
    width = rows_ref.shape[1]
    half = width // 2
    full = packed // width
    eight = 8 * peers
    chunks = FF // COLS
    copies = []
    for j in range(chunks):
        for start in (j * COLS, FF + j * COLS):
            part = (slice(None), pl.ds(start, COLS))
            copies.append(
                pltpu.make_async_copy(gu_hbm.at[part], gu_ref.at[part], sems.at[len(copies)])
            )
    copies.append(pltpu.make_async_copy(down_hbm, down_ref, sems.at[len(copies)]))

    @pl.when(step == 0)
    def _():
        for copy in copies:
            copy.start()

    for q in range(0, peers, 4):
        for g in range(full):
            rows_ref[pl.ds(g * eight + 8 * q, 32), :] = in_rows(
                x_ref[q : q + 4, :, g * width : (g + 1) * width]
            )
        if packed > full * width:
            fold = [x_ref[p, :, full * width :].astype(jnp.float32) for p in range(q, q + 4)]
            for part, first in ((0, 0), (1, 4)):
                rows_ref[pl.ds(full * eight + 4 * q, 16), pl.ds(part * half, half)] = (
                    jnp.concatenate([f[first : first + 4] for f in fold], axis=0)
                ).astype(jnp.bfloat16)

    for j in range(chunks):

        @pl.when(step == 0)
        def _():
            copies[2 * j].wait()
            copies[2 * j + 1].wait()

        gate = jnp.dot(
            rows_ref[...], gu_ref[:, j * COLS : (j + 1) * COLS], preferred_element_type=jnp.float32
        )
        up = jnp.dot(
            rows_ref[...],
            gu_ref[:, FF + j * COLS : FF + (j + 1) * COLS],
            preferred_element_type=jnp.float32,
        )
        active_ref[:, j * COLS : (j + 1) * COLS] = (gate / (1.0 + jnp.exp(-gate)) * up).astype(
            jnp.bfloat16
        )

    @pl.when(step == 0)
    def _():
        copies[-1].wait()

    for j in range(half // COLS):
        sides = []
        for side in range(2):
            at = side * half + j * COLS
            y = jnp.dot(
                active_ref[...], down_ref[:, at : at + COLS], preferred_element_type=jnp.float32
            )
            sides.append(y)
            for g in range(full):
                to = place + g * width + at
                out_ref[:, :, to : to + COLS] = (
                    y[g * eight : (g + 1) * eight].reshape(peers, 8, COLS).astype(jnp.bfloat16)
                )
        if packed > full * width:
            for p in range(peers):
                at = full * eight + 4 * p
                to = place + full * width + j * COLS
                out_ref[p, :, to : to + COLS] = (
                    jnp.concatenate([sides[0][at : at + 4], sides[1][at : at + 4]], axis=0)
                ).astype(jnp.bfloat16)


def run_expert(arrived, w_gu, w_down, place, produced=None):
    peers, _, packed = arrived.shape
    width = w_gu.shape[0]
    each = 8 * packed // width
    group = 32
    rows = peers * each
    total = width * 5 // 2
    columns = total if produced is None else packed
    before = () if produced is None else (produced,)
    return pl.pallas_call(
        functools.partial(expert_kernel, place),
        grid=(peers // group,),
        in_specs=[
            pl.BlockSpec((group, 8, packed), lambda i: (i, 0, 0)),
            pl.BlockSpec(memory_space=pl.ANY),
            pl.BlockSpec(memory_space=pl.ANY),
        ]
        + [pl.BlockSpec(memory_space=pl.ANY)] * len(before),
        out_specs=pl.BlockSpec((group, 8, columns), lambda i: (i, 0, 0)),
        out_shape=jax.ShapeDtypeStruct((peers, 8, total), jnp.bfloat16),
        input_output_aliases={3: 0} if before else {},
        scratch_shapes=[
            pltpu.VMEM(w_gu.shape, jnp.bfloat16),
            pltpu.VMEM(w_down.shape, jnp.bfloat16),
            pltpu.VMEM((group * each, width), jnp.bfloat16),
            pltpu.VMEM((group * each, FF), jnp.bfloat16),
            pltpu.SemaphoreType.DMA((2 * FF // COLS + 1,)),
        ],
        compiler_params=pltpu.CompilerParams(vmem_limit_bytes=58 * 1024 * 1024),
        cost_estimate=pl.CostEstimate(
            flops=rows * width * FF * 6,
            bytes_accessed=rows * width * 4 + width * FF * 6,
            transcendentals=rows * FF,
        ),
        name="run_expert",
    )(arrived, w_gu, w_down, *before)


def combine_kernel(x_ref, rank_ref, gate_ref, cotangent_ref, out_ref, grad_ref, sum_ref):
    step = pl.program_id(0)
    tokens, width = cotangent_ref.shape
    half = width // 2

    @pl.when(step == 0)
    def _():
        sum_ref[...] = jnp.zeros_like(sum_ref)

    rank = rank_ref[...][:, None, :]
    gate = gate_ref[...][:, None, :]
    shape = (GROUP, 8, tokens)
    row = lax.broadcasted_iota(jnp.int32, shape, 1)
    low = row < 4
    pieces = [
        (rank == row, 0, 0, width),
        (rank == row + 8, width, 0, width),
        ((rank == row + 16) & low, 2 * width, 0, half),
        ((rank == row + 12) & ~low, 2 * width, half, half),
    ]
    grad = jnp.zeros((GROUP, tokens), jnp.float32)
    for mask, source, place, count in pieces:
        rows = in_rows(x_ref[:, :, source : source + count])
        weight = jnp.where(mask, gate, 0.0).reshape(-1, tokens).astype(jnp.bfloat16)
        sum_ref[:, place : place + count] += lax.dot_general(
            weight, rows, (((0,), (0,)), ((), ())), preferred_element_type=jnp.float32
        )
        inner = lax.dot_general(
            rows,
            cotangent_ref[:, place : place + count],
            (((1,), (1,)), ((), ())),
            preferred_element_type=jnp.float32,
        )
        grad += jnp.sum(jnp.where(mask, inner.reshape(shape), 0.0), axis=1)
    grad_ref[...] = grad

    @pl.when(step == pl.num_programs(0) - 1)
    def _():
        out_ref[...] = sum_ref[...].astype(jnp.bfloat16)


def combine(returned, rank, gate_of, cotangent):
    peers, _, packed = returned.shape
    tokens, width = cotangent.shape
    return pl.pallas_call(
        combine_kernel,
        grid=(peers // GROUP,),
        in_specs=[
            pl.BlockSpec((GROUP, 8, packed), lambda i: (i, 0, 0)),
            pl.BlockSpec((GROUP, tokens), lambda i: (i, 0)),
            pl.BlockSpec((GROUP, tokens), lambda i: (i, 0)),
            pl.BlockSpec((tokens, width), lambda i: (0, 0)),
        ],
        out_specs=[
            pl.BlockSpec((tokens, width), lambda i: (0, 0)),
            pl.BlockSpec((GROUP, tokens), lambda i: (i, 0)),
        ],
        out_shape=[
            jax.ShapeDtypeStruct((tokens, width), jnp.bfloat16),
            jax.ShapeDtypeStruct((peers, tokens), jnp.float32),
        ],
        scratch_shapes=[pltpu.VMEM((tokens, width), jnp.float32)],
        compiler_params=pltpu.CompilerParams(vmem_limit_bytes=40 * 1024 * 1024),
        cost_estimate=pl.CostEstimate(
            flops=peers * 24 * tokens * width * 4,
            bytes_accessed=peers * 40 * width + tokens * width * 4,
            transcendentals=0,
        ),
        name="combine",
    )(returned, rank, gate_of, cotangent)


def shards(
    tokens, cotangent, routes, gates, previous_row, gu_payload, gu_scales, down_payload, down_scales
):
    local_count, model_width = tokens.shape
    half = model_width // 2
    devices = lax.axis_size("expert")
    experts = previous_row.shape[0]
    device_id = lax.axis_index("expert")
    chip, core = device_id // 2, device_id % 2
    parity = core.astype(jnp.int32).reshape(1)
    same_core = [[2 * c + p for c in range(experts)] for p in range(2)]
    swap = [(d, d ^ 1) for d in range(devices)]

    def exchange(x):
        return lax.all_to_all(x, "expert", 0, 0, axis_index_groups=same_core, tiled=True)

    down_own = exchange(down_payload)
    packed = jnp.concatenate(
        [lax.dynamic_slice_in_dim(gu_payload, 4 * core + 8 * g, 8, axis=1) for g in range(3)]
        + [
            jnp.concatenate(
                [
                    lax.dynamic_slice_in_dim(gu_payload[:, :, half_ff : half_ff + FF], 24 - 24 * core, 4, axis=1)
                    for half_ff in (0, FF)
                ],
                axis=1,
            )
        ],
        axis=2,
    )
    gu_scale = jnp.repeat(gu_scales[chip], 128, axis=1)
    down_scale = jnp.repeat(down_scales[chip], 128, axis=1)

    routes_t = routes.T
    gates_t = gates.T.astype(jnp.float32)
    slots = jnp.arange(experts, dtype=jnp.int32)[None, :, None]
    target = jnp.sum(
        jnp.where(routes_t[:, None, :] == slots, previous_row[None, :, None], 0), axis=1
    )
    named = target[:, None, :] == slots
    member = jnp.any(named, axis=0)
    gate_of = jnp.sum(jnp.where(named, gates_t[:, None, :], 0.0), axis=0)
    earlier = jnp.arange(local_count)[:, None] < jnp.arange(local_count)[None, :]
    rank = jnp.dot(
        member.astype(jnp.bfloat16), earlier.astype(jnp.bfloat16), preferred_element_type=jnp.float32
    ).astype(jnp.int32)
    rank = jnp.where(member, rank, -1)

    def picked(places):
        select = (rank[:, None, :] == places[None, :, None]).astype(jnp.bfloat16)
        rows = jnp.dot(
            select.reshape(-1, local_count), tokens, preferred_element_type=jnp.float32
        ).astype(jnp.bfloat16)
        return rows.reshape(experts, places.shape[0], model_width)

    eight = jnp.arange(8, dtype=jnp.int32)
    outgoing_a = picked(eight)
    last = picked(16 + eight % 4)
    last = jnp.where(eight[None, :, None] < 4, last[:, :, :half], last[:, :, half:])
    outgoing_b = jnp.concatenate([picked(8 + eight), last], axis=2)

    packed, outgoing_a, outgoing_b, down_own, rank, gate_of, gu_scale, down_scale = (
        lax.optimization_barrier(
            (packed, outgoing_a, outgoing_b, down_own, rank, gate_of, gu_scale, down_scale)
        )
    )
    gu_own = exchange(packed)
    gu_own, outgoing_b = lax.optimization_barrier((gu_own, outgoing_b))
    gu_other = lax.ppermute(gu_own, "expert", swap)
    arrived_b = exchange(outgoing_b)
    arrived_b, gu_other, down_own, outgoing_a = lax.optimization_barrier(
        (arrived_b, gu_other, down_own, outgoing_a)
    )
    arrived_a = exchange(outgoing_a)
    down_other = lax.ppermute(down_own, "expert", swap)
    w_gu = dequantize_gu(gu_own, gu_other, gu_scale, parity)
    w_down = dequantize_down(down_own, down_other, down_scale, parity)
    produced = run_expert(arrived_b, w_gu, w_down, model_width)
    produced, arrived_a = lax.optimization_barrier((produced, arrived_a))
    produced = run_expert(arrived_a, w_gu, w_down, 0, produced)
    returned = exchange(produced)
    layer_out, grad = combine(returned, rank, gate_of, cotangent)
    gate_grad = jnp.sum(jnp.where(named, grad[None], 0.0), axis=1).T
    return (layer_out, gate_grad)


def solution(mesh):
    in_specs = (
        P("expert", None),
        P("expert", None),
        P("expert", None),
        P("expert", None),
        P(),
        P(None, "expert", None),
        P(),
        P(None, "expert", None),
        P(),
    )
    out_specs = (P("expert", None), P("expert", None))
    return jax.shard_map(shards, mesh=mesh, in_specs=in_specs, out_specs=out_specs, check_vma=False)
```

```python
import functools

import jax
import jax.numpy as jnp
from jax import lax
from jax.experimental import pallas as pl
from jax.experimental.pallas import tpu as pltpu
from jax.sharding import PartitionSpec as P

FF = 1024
TOP = 8
COLS = 256
GROUP = 16


def in_rows(block):
    return block.reshape(-1, block.shape[-1])


def by_core(parity_ref, own_ref, other_ref, body):
    @pl.when(parity_ref[0] == 0)
    def _():
        body(own_ref, other_ref)

    @pl.when(parity_ref[0] != 0)
    def _():
        body(other_ref, own_ref)


def gu_kernel(parity_ref, own_ref, other_ref, scale_ref, out_ref):
    step = pl.program_id(0)
    width = out_ref.shape[1]

    def body(zero_ref, one_ref):
        tiles = []
        for chip in range(zero_ref.shape[0]):
            zero = [zero_ref[chip, :, g * width : (g + 1) * width] for g in range(3)]
            one = [one_ref[chip, :, g * width : (g + 1) * width] for g in range(3)]
            fold_zero = zero_ref[chip, :, 3 * width :].astype(jnp.float32)
            fold_one = one_ref[chip, :, 3 * width :].astype(jnp.float32)
            middle = jnp.concatenate(
                [
                    jnp.concatenate([fold_zero[:4], fold_one[:4]], axis=0),
                    jnp.concatenate([fold_zero[4:], fold_one[4:]], axis=0),
                ],
                axis=1,
            )
            tiles += zero + [middle] + one
        for pair in range(len(tiles) // 2):
            scaled = []
            for k in (2 * pair, 2 * pair + 1):
                at = (step * 8 * len(tiles) + 8 * k) // 128
                scaled.append(tiles[k].astype(jnp.float32) * scale_ref[pl.ds(at, 1), :])
            out_ref[16 * pair : 16 * pair + 16, :] = jnp.concatenate(scaled, axis=0).astype(
                jnp.bfloat16
            )

    by_core(parity_ref, own_ref, other_ref, body)


def dequantize_gu(own, other, scales, parity):
    chips, _, packed = own.shape
    width = 2 * FF
    return pl.pallas_call(
        gu_kernel,
        grid=(chips // 2,),
        in_specs=[
            pl.BlockSpec(memory_space=pltpu.SMEM),
            pl.BlockSpec((2, 8, packed), lambda i: (i, 0, 0)),
            pl.BlockSpec((2, 8, packed), lambda i: (i, 0, 0)),
            pl.BlockSpec(scales.shape, lambda i: (0, 0)),
        ],
        out_specs=pl.BlockSpec((112, width), lambda i: (i, 0)),
        out_shape=jax.ShapeDtypeStruct((chips * 56, width), jnp.bfloat16),
        compiler_params=pltpu.CompilerParams(vmem_limit_bytes=60 * 1024 * 1024),
        cost_estimate=pl.CostEstimate(
            flops=chips * 56 * width, bytes_accessed=chips * 56 * width * 4, transcendentals=0
        ),
        name="dequantize_gu",
    )(parity, own, other, scales)


def down_kernel(parity_ref, own_ref, other_ref, scale_ref, out_ref):
    step = pl.program_id(0)
    chips = own_ref.shape[0]
    scale = scale_ref[pl.ds(step * chips * 16 // 128, 1), :]

    def body(zero_ref, one_ref):
        for chip in range(chips):
            both = [ref[chip].astype(jnp.float32) * scale for ref in (zero_ref, one_ref)]
            out_ref[16 * chip : 16 * chip + 16, :] = jnp.concatenate(both, axis=0).astype(
                jnp.bfloat16
            )

    by_core(parity_ref, own_ref, other_ref, body)


def dequantize_down(own, other, scales, parity):
    chips, _, width = own.shape
    return pl.pallas_call(
        down_kernel,
        grid=(chips // 8,),
        in_specs=[
            pl.BlockSpec(memory_space=pltpu.SMEM),
            pl.BlockSpec((8, 8, width), lambda i: (i, 0, 0)),
            pl.BlockSpec((8, 8, width), lambda i: (i, 0, 0)),
            pl.BlockSpec(scales.shape, lambda i: (0, 0)),
        ],
        out_specs=pl.BlockSpec((128, width), lambda i: (i, 0)),
        out_shape=jax.ShapeDtypeStruct((chips * 16, width), jnp.bfloat16),
        compiler_params=pltpu.CompilerParams(vmem_limit_bytes=60 * 1024 * 1024),
        cost_estimate=pl.CostEstimate(
            flops=chips * 16 * width, bytes_accessed=chips * 16 * width * 4, transcendentals=0
        ),
        name="dequantize_down",
    )(parity, own, other, scales)


def expert_kernel(place, x_hbm, gu_hbm, down_hbm, *refs):
    out_hbm, x_ref, gu_ref, down_ref, rows_ref, active_ref, back_ref, in_sems, out_sems = refs[-9:]
    peers, _, packed = x_ref.shape
    width = rows_ref.shape[1]
    half = width // 2
    full = packed // width
    eight = 8 * peers
    chunks = FF // COLS
    arrivals, weights = [], []
    for q in range(0, peers, GROUP):
        part = pl.ds(q, GROUP)
        arrivals.append(pltpu.make_async_copy(x_hbm.at[part], x_ref.at[part], in_sems.at[len(arrivals)]))
    for j in range(chunks):
        for start in (j * COLS, FF + j * COLS):
            part = (slice(None), pl.ds(start, COLS))
            sem = in_sems.at[len(arrivals) + len(weights)]
            weights.append(pltpu.make_async_copy(gu_hbm.at[part], gu_ref.at[part], sem))
    for side in range(2):
        part = (slice(None), pl.ds(side * half, half))
        sem = in_sems.at[len(arrivals) + len(weights)]
        weights.append(pltpu.make_async_copy(down_hbm.at[part], down_ref.at[part], sem))
    for copy in arrivals + weights:
        copy.start()

    for q in range(0, peers, 4):
        if q % GROUP == 0:
            arrivals[q // GROUP].wait()
        for g in range(full):
            rows_ref[pl.ds(g * eight + 8 * q, 32), :] = in_rows(
                x_ref[q : q + 4, :, g * width : (g + 1) * width]
            )
        if packed > full * width:
            fold = [x_ref[p, :, full * width :].astype(jnp.float32) for p in range(q, q + 4)]
            for part, first in ((0, 0), (1, 4)):
                rows_ref[pl.ds(full * eight + 4 * q, 16), pl.ds(part * half, half)] = (
                    jnp.concatenate([f[first : first + 4] for f in fold], axis=0)
                ).astype(jnp.bfloat16)

    for j in range(chunks):
        weights[2 * j].wait()
        gate = jnp.dot(
            rows_ref[...], gu_ref[:, j * COLS : (j + 1) * COLS], preferred_element_type=jnp.float32
        )
        weights[2 * j + 1].wait()
        up = jnp.dot(
            rows_ref[...],
            gu_ref[:, FF + j * COLS : FF + (j + 1) * COLS],
            preferred_element_type=jnp.float32,
        )
        active_ref[:, j * COLS : (j + 1) * COLS] = (gate / (1.0 + jnp.exp(-gate)) * up).astype(
            jnp.bfloat16
        )

    weights[-2].wait()
    weights[-1].wait()
    leaving = []

    def leave(start):
        copy = pltpu.make_async_copy(
            back_ref.at[:, :, pl.ds(start, COLS)],
            out_hbm.at[:, :, pl.ds(place + start, COLS)],
            out_sems.at[len(leaving)],
        )
        copy.start()
        leaving.append(copy)

    for j in range(half // COLS):
        sides = []
        for side in range(2):
            at = side * half + j * COLS
            y = jnp.dot(
                active_ref[...], down_ref[:, at : at + COLS], preferred_element_type=jnp.float32
            )
            sides.append(y)
            for g in range(full):
                to = g * width + at
                back_ref[:, :, to : to + COLS] = (
                    y[g * eight : (g + 1) * eight].reshape(peers, 8, COLS).astype(jnp.bfloat16)
                )
                leave(to)
        if packed > full * width:
            to = full * width + j * COLS
            for p in range(peers):
                at = full * eight + 4 * p
                back_ref[p, :, to : to + COLS] = (
                    jnp.concatenate([sides[0][at : at + 4], sides[1][at : at + 4]], axis=0)
                ).astype(jnp.bfloat16)
            leave(to)
    for copy in leaving:
        copy.wait()


def run_expert(arrived, w_gu, w_down, place, produced=None):
    peers, _, packed = arrived.shape
    width = w_gu.shape[0]
    rows = peers * (8 * packed // width)
    total = width * 5 // 2
    before = () if produced is None else (produced,)
    return pl.pallas_call(
        functools.partial(expert_kernel, place),
        in_specs=[pl.BlockSpec(memory_space=pl.ANY)] * (3 + len(before)),
        out_specs=pl.BlockSpec(memory_space=pl.ANY),
        out_shape=jax.ShapeDtypeStruct((peers, 8, total), jnp.bfloat16),
        input_output_aliases={3: 0} if before else {},
        scratch_shapes=[
            pltpu.VMEM(arrived.shape, jnp.bfloat16),
            pltpu.VMEM(w_gu.shape, jnp.bfloat16),
            pltpu.VMEM(w_down.shape, jnp.bfloat16),
            pltpu.VMEM((rows, width), jnp.bfloat16),
            pltpu.VMEM((rows, FF), jnp.bfloat16),
            pltpu.VMEM(arrived.shape, jnp.bfloat16),
            pltpu.SemaphoreType.DMA((peers // GROUP + 2 * FF // COLS + 2,)),
            pltpu.SemaphoreType.DMA((packed // COLS,)),
        ],
        compiler_params=pltpu.CompilerParams(vmem_limit_bytes=60 * 1024 * 1024),
        cost_estimate=pl.CostEstimate(
            flops=rows * width * FF * 6,
            bytes_accessed=rows * width * 4 + width * FF * 6,
            transcendentals=rows * FF,
        ),
        name="run_expert",
    )(arrived, w_gu, w_down, *before)


def combine_kernel(x_ref, rank_ref, gate_ref, cotangent_ref, out_ref, grad_ref, sum_ref):
    step = pl.program_id(0)
    tokens, width = cotangent_ref.shape
    half = width // 2

    @pl.when(step == 0)
    def _():
        sum_ref[...] = jnp.zeros_like(sum_ref)

    rank = rank_ref[...][:, None, :]
    gate = gate_ref[...][:, None, :]
    shape = (GROUP, 8, tokens)
    row = lax.broadcasted_iota(jnp.int32, shape, 1)
    low = row < 4
    pieces = [
        (rank == row, 0, 0, width),
        (rank == row + 8, width, 0, width),
        ((rank == row + 16) & low, 2 * width, 0, half),
        ((rank == row + 12) & ~low, 2 * width, half, half),
    ]
    grad = jnp.zeros((GROUP, tokens), jnp.float32)
    for mask, source, place, count in pieces:
        rows = in_rows(x_ref[:, :, source : source + count])
        weight = jnp.where(mask, gate, 0.0).reshape(-1, tokens).astype(jnp.bfloat16)
        sum_ref[:, place : place + count] += lax.dot_general(
            weight, rows, (((0,), (0,)), ((), ())), preferred_element_type=jnp.float32
        )
        inner = lax.dot_general(
            rows,
            cotangent_ref[:, place : place + count],
            (((1,), (1,)), ((), ())),
            preferred_element_type=jnp.float32,
        )
        grad += jnp.sum(jnp.where(mask, inner.reshape(shape), 0.0), axis=1)
    grad_ref[...] = grad

    @pl.when(step == pl.num_programs(0) - 1)
    def _():
        out_ref[...] = sum_ref[...].astype(jnp.bfloat16)


def combine(returned, rank, gate_of, cotangent):
    peers, _, packed = returned.shape
    tokens, width = cotangent.shape
    return pl.pallas_call(
        combine_kernel,
        grid=(peers // GROUP,),
        in_specs=[
            pl.BlockSpec((GROUP, 8, packed), lambda i: (i, 0, 0)),
            pl.BlockSpec((GROUP, tokens), lambda i: (i, 0)),
            pl.BlockSpec((GROUP, tokens), lambda i: (i, 0)),
            pl.BlockSpec((tokens, width), lambda i: (0, 0)),
        ],
        out_specs=[
            pl.BlockSpec((tokens, width), lambda i: (0, 0)),
            pl.BlockSpec((GROUP, tokens), lambda i: (i, 0)),
        ],
        out_shape=[
            jax.ShapeDtypeStruct((tokens, width), jnp.bfloat16),
            jax.ShapeDtypeStruct((peers, tokens), jnp.float32),
        ],
        scratch_shapes=[pltpu.VMEM((tokens, width), jnp.float32)],
        compiler_params=pltpu.CompilerParams(vmem_limit_bytes=56 * 1024 * 1024),
        cost_estimate=pl.CostEstimate(
            flops=peers * 24 * tokens * width * 4,
            bytes_accessed=peers * 40 * width + tokens * width * 4,
            transcendentals=0,
        ),
        name="combine",
    )(returned, rank, gate_of, cotangent)


def shards(
    tokens, cotangent, routes, gates, previous_row, gu_payload, gu_scales, down_payload, down_scales
):
    local_count, model_width = tokens.shape
    half = model_width // 2
    devices = lax.axis_size("expert")
    experts = previous_row.shape[0]
    device_id = lax.axis_index("expert")
    chip, core = device_id // 2, device_id % 2
    parity = core.astype(jnp.int32).reshape(1)
    same_core = [[2 * c + p for c in range(experts)] for p in range(2)]
    swap = [(d, d ^ 1) for d in range(devices)]

    def exchange(x):
        return lax.all_to_all(x, "expert", 0, 0, axis_index_groups=same_core, tiled=True)

    down_own = exchange(down_payload)
    packed = jnp.concatenate(
        [lax.dynamic_slice_in_dim(gu_payload, 4 * core + 8 * g, 8, axis=1) for g in range(3)]
        + [
            jnp.concatenate(
                [
                    lax.dynamic_slice_in_dim(gu_payload[:, :, half_ff : half_ff + FF], 24 - 24 * core, 4, axis=1)
                    for half_ff in (0, FF)
                ],
                axis=1,
            )
        ],
        axis=2,
    )
    gu_scale = jnp.repeat(gu_scales[chip], 128, axis=1)
    down_scale = jnp.repeat(down_scales[chip], 128, axis=1)

    routes_t = routes.T
    gates_t = gates.T.astype(jnp.float32)
    slots = jnp.arange(experts, dtype=jnp.int32)[None, :, None]
    target = jnp.sum(
        jnp.where(routes_t[:, None, :] == slots, previous_row[None, :, None], 0), axis=1
    )
    named = target[:, None, :] == slots
    member = jnp.any(named, axis=0)
    gate_of = jnp.sum(jnp.where(named, gates_t[:, None, :], 0.0), axis=0)
    earlier = jnp.arange(local_count)[:, None] < jnp.arange(local_count)[None, :]
    rank = jnp.dot(
        member.astype(jnp.bfloat16), earlier.astype(jnp.bfloat16), preferred_element_type=jnp.float32
    ).astype(jnp.int32)
    rank = jnp.where(member, rank, -1)

    def picked(places):
        select = (rank[:, None, :] == places[None, :, None]).astype(jnp.bfloat16)
        rows = jnp.dot(
            select.reshape(-1, local_count), tokens, preferred_element_type=jnp.float32
        ).astype(jnp.bfloat16)
        return rows.reshape(experts, places.shape[0], model_width)

    eight = jnp.arange(8, dtype=jnp.int32)
    outgoing_a = picked(eight)
    last = picked(16 + eight % 4)
    last = jnp.where(eight[None, :, None] < 4, last[:, :, :half], last[:, :, half:])
    outgoing_b = jnp.concatenate([picked(8 + eight), last], axis=2)

    packed, outgoing_a, outgoing_b, down_own, rank, gate_of, gu_scale, down_scale = (
        lax.optimization_barrier(
            (packed, outgoing_a, outgoing_b, down_own, rank, gate_of, gu_scale, down_scale)
        )
    )
    gu_own = exchange(packed)
    gu_own, outgoing_b = lax.optimization_barrier((gu_own, outgoing_b))
    gu_other = lax.ppermute(gu_own, "expert", swap)
    arrived_b = exchange(outgoing_b)
    arrived_b, gu_other, down_own, outgoing_a = lax.optimization_barrier(
        (arrived_b, gu_other, down_own, outgoing_a)
    )
    arrived_a = exchange(outgoing_a)
    down_other = lax.ppermute(down_own, "expert", swap)
    w_gu = dequantize_gu(gu_own, gu_other, gu_scale, parity)
    w_down = dequantize_down(down_own, down_other, down_scale, parity)
    produced = run_expert(arrived_b, w_gu, w_down, model_width)
    produced, arrived_a = lax.optimization_barrier((produced, arrived_a))
    produced = run_expert(arrived_a, w_gu, w_down, 0, produced)
    returned = exchange(produced)
    layer_out, grad = combine(returned, rank, gate_of, cotangent)
    gate_grad = jnp.sum(jnp.where(named, grad[None], 0.0), axis=1).T
    return (layer_out, gate_grad)


def solution(mesh):
    in_specs = (
        P("expert", None),
        P("expert", None),
        P("expert", None),
        P("expert", None),
        P(),
        P(None, "expert", None),
        P(),
        P(None, "expert", None),
        P(),
    )
    out_specs = (P("expert", None), P("expert", None))
    return jax.shard_map(shards, mesh=mesh, in_specs=in_specs, out_specs=out_specs, check_vma=False)
```

```python
import functools

import jax
import jax.numpy as jnp
from jax import lax
from jax.experimental import pallas as pl
from jax.experimental.pallas import tpu as pltpu
from jax.sharding import PartitionSpec as P

FF = 1024
TOP = 8
COLS = 256
GROUP = 16


def in_rows(block):
    return block.astype(jnp.float32).reshape(-1, block.shape[-1]).astype(jnp.bfloat16)


def restore(zero_gu, one_gu, zero_down, one_down, gu_scale_ref, down_scale_ref, step, gu_ref, down_ref):
    width = gu_ref.shape[1]
    chips = zero_gu.shape[0]
    tiles = []
    for chip in range(chips):
        zero = [zero_gu[chip, :, g * width : (g + 1) * width] for g in range(3)]
        one = [one_gu[chip, :, g * width : (g + 1) * width] for g in range(3)]
        fold_zero = zero_gu[chip, :, 3 * width :].astype(jnp.float32)
        fold_one = one_gu[chip, :, 3 * width :].astype(jnp.float32)
        middle = jnp.concatenate(
            [
                jnp.concatenate([fold_zero[:4], fold_one[:4]], axis=0),
                jnp.concatenate([fold_zero[4:], fold_one[4:]], axis=0),
            ],
            axis=1,
        )
        tiles += zero + [middle] + one
    for pair in range(len(tiles) // 2):
        scaled = []
        for k in (2 * pair, 2 * pair + 1):
            at = (step * 8 * len(tiles) + 8 * k) // 128
            scaled.append(tiles[k].astype(jnp.float32) * gu_scale_ref[pl.ds(at, 1), :])
        start = pl.multiple_of(step * 8 * len(tiles) + 16 * pair, 16)
        gu_ref[pl.ds(start, 16), :] = jnp.concatenate(scaled, axis=0).astype(jnp.bfloat16)
    scale = down_scale_ref[pl.ds(step * chips * 16 // 128, 1), :]
    for chip in range(chips):
        both = [ref[chip].astype(jnp.float32) * scale for ref in (zero_down, one_down)]
        start = pl.multiple_of((step * chips + chip) * 16, 16)
        down_ref[pl.ds(start, 16), :] = jnp.concatenate(both, axis=0).astype(jnp.bfloat16)


def expert_rows(place, x_ref, out_ref, gu_ref, down_ref, rows_ref, active_ref, ready):
    peers, _, packed = x_ref.shape
    width = rows_ref.shape[1]
    half = width // 2
    full = packed // width
    eight = 8 * peers
    chunks = FF // COLS

    for q in range(0, peers, 4):
        for g in range(full):
            rows_ref[pl.ds(g * eight + 8 * q, 32), :] = in_rows(
                x_ref[q : q + 4, :, g * width : (g + 1) * width]
            )
        if packed > full * width:
            fold = [x_ref[p, :, full * width :].astype(jnp.float32) for p in range(q, q + 4)]
            for part, first in ((0, 0), (1, 4)):
                rows_ref[pl.ds(full * eight + 4 * q, 16), pl.ds(part * half, half)] = (
                    jnp.concatenate([f[first : first + 4] for f in fold], axis=0)
                ).astype(jnp.bfloat16)

    for j in range(chunks):
        ready(j)
        gate = jnp.dot(
            rows_ref[...], gu_ref[:, j * COLS : (j + 1) * COLS], preferred_element_type=jnp.float32
        )
        up = jnp.dot(
            rows_ref[...],
            gu_ref[:, FF + j * COLS : FF + (j + 1) * COLS],
            preferred_element_type=jnp.float32,
        )
        active_ref[:, j * COLS : (j + 1) * COLS] = (gate / (1.0 + jnp.exp(-gate)) * up).astype(
            jnp.bfloat16
        )
    ready(chunks)

    for j in range(half // COLS):
        sides = []
        for side in range(2):
            at = side * half + j * COLS
            y = jnp.dot(
                active_ref[...], down_ref[:, at : at + COLS], preferred_element_type=jnp.float32
            )
            sides.append(y)
            for g in range(full):
                to = place + g * width + at
                out_ref[:, :, to : to + COLS] = (
                    y[g * eight : (g + 1) * eight].reshape(peers, 8, COLS).astype(jnp.bfloat16)
                )
        if packed > full * width:
            for p in range(peers):
                at = full * eight + 4 * p
                to = place + full * width + j * COLS
                out_ref[p, :, to : to + COLS] = (
                    jnp.concatenate([sides[0][at : at + 4], sides[1][at : at + 4]], axis=0)
                ).astype(jnp.bfloat16)


def first_kernel(place, parity_ref, own_gu, other_gu, own_down, other_down, gu_scale_ref, down_scale_ref, x_ref, out_ref, gu_hbm, down_hbm, gu_ref, down_ref, rows_ref, active_ref, sems):
    step = pl.program_id(0)
    restoring = gu_ref.shape[0] // (56 * own_gu.shape[0])
    scales = (gu_scale_ref, down_scale_ref)

    @pl.when((step < restoring) & (parity_ref[0] == 0))
    def _():
        restore(own_gu, other_gu, own_down, other_down, *scales, step, gu_ref, down_ref)

    @pl.when((step < restoring) & (parity_ref[0] != 0))
    def _():
        restore(other_gu, own_gu, other_down, own_down, *scales, step, gu_ref, down_ref)

    leaving = [
        pltpu.make_async_copy(gu_ref, gu_hbm, sems.at[0]),
        pltpu.make_async_copy(down_ref, down_hbm, sems.at[1]),
    ]

    @pl.when(step == restoring)
    def _():
        for copy in leaving:
            copy.start()

    @pl.when(step >= restoring)
    def _():
        expert_rows(place, x_ref, out_ref, gu_ref, down_ref, rows_ref, active_ref, lambda j: None)

    @pl.when(step == pl.num_programs(0) - 1)
    def _():
        for copy in leaving:
            copy.wait()


def run_first(arrived, own_gu, other_gu, own_down, other_down, gu_scale, down_scale, parity, place):
    peers, _, packed = arrived.shape
    width = down_scale.shape[1]
    each = 8 * packed // width
    total = width * 5 // 2
    group, chips = 32, 4
    restoring = peers // chips
    rows = peers * each

    def part(count):
        return pl.BlockSpec((chips, 8, count), lambda i: (jnp.minimum(i, restoring - 1), 0, 0))

    def piece(count):
        return pl.BlockSpec((group, 8, count), lambda i: (jnp.maximum(i - restoring, 0), 0, 0))

    gu_shape, down_shape = (width, 2 * FF), (FF, width)
    return pl.pallas_call(
        functools.partial(first_kernel, place),
        grid=(restoring + peers // group,),
        in_specs=[
            pl.BlockSpec(memory_space=pltpu.SMEM),
            part(own_gu.shape[2]),
            part(own_gu.shape[2]),
            part(width),
            part(width),
            pl.BlockSpec(gu_scale.shape, lambda i: (0, 0)),
            pl.BlockSpec(down_scale.shape, lambda i: (0, 0)),
            piece(packed),
        ],
        out_specs=[piece(total), pl.BlockSpec(memory_space=pl.ANY), pl.BlockSpec(memory_space=pl.ANY)],
        out_shape=[
            jax.ShapeDtypeStruct((peers, 8, total), jnp.bfloat16),
            jax.ShapeDtypeStruct(gu_shape, jnp.bfloat16),
            jax.ShapeDtypeStruct(down_shape, jnp.bfloat16),
        ],
        scratch_shapes=[
            pltpu.VMEM(gu_shape, jnp.bfloat16),
            pltpu.VMEM(down_shape, jnp.bfloat16),
            pltpu.VMEM((group * each, width), jnp.bfloat16),
            pltpu.VMEM((group * each, FF), jnp.bfloat16),
            pltpu.SemaphoreType.DMA((2,)),
        ],
        compiler_params=pltpu.CompilerParams(vmem_limit_bytes=56 * 1024 * 1024),
        cost_estimate=pl.CostEstimate(
            flops=rows * width * FF * 6,
            bytes_accessed=rows * width * 4 + width * FF * 12,
            transcendentals=rows * FF,
        ),
        name="restore_and_run",
    )(parity, own_gu, other_gu, own_down, other_down, gu_scale, down_scale, arrived)


def expert_kernel(x_ref, gu_hbm, down_hbm, produced, out_ref, gu_ref, down_ref, rows_ref, active_ref, sems):
    step = pl.program_id(0)
    copies = []
    for j in range(FF // COLS):
        for start in (j * COLS, FF + j * COLS):
            part = (slice(None), pl.ds(start, COLS))
            copies.append(
                pltpu.make_async_copy(gu_hbm.at[part], gu_ref.at[part], sems.at[len(copies)])
            )
    copies.append(pltpu.make_async_copy(down_hbm, down_ref, sems.at[len(copies)]))

    @pl.when(step == 0)
    def _():
        for copy in copies:
            copy.start()

    def ready(j):
        @pl.when(step == 0)
        def _():
            for copy in copies[2 * j : 2 * j + 2]:
                copy.wait()

    expert_rows(0, x_ref, out_ref, gu_ref, down_ref, rows_ref, active_ref, ready)


def run_expert(arrived, w_gu, w_down, produced):
    peers, _, packed = arrived.shape
    width = w_gu.shape[0]
    each = 8 * packed // width
    group = 64
    rows = peers * each
    piece = pl.BlockSpec((group, 8, packed), lambda i: (i, 0, 0))
    return pl.pallas_call(
        expert_kernel,
        grid=(peers // group,),
        in_specs=[piece] + [pl.BlockSpec(memory_space=pl.ANY)] * 3,
        out_specs=piece,
        out_shape=jax.ShapeDtypeStruct(produced.shape, jnp.bfloat16),
        input_output_aliases={3: 0},
        scratch_shapes=[
            pltpu.VMEM(w_gu.shape, jnp.bfloat16),
            pltpu.VMEM(w_down.shape, jnp.bfloat16),
            pltpu.VMEM((group * each, width), jnp.bfloat16),
            pltpu.VMEM((group * each, FF), jnp.bfloat16),
            pltpu.SemaphoreType.DMA((2 * FF // COLS + 1,)),
        ],
        compiler_params=pltpu.CompilerParams(vmem_limit_bytes=58 * 1024 * 1024),
        cost_estimate=pl.CostEstimate(
            flops=rows * width * FF * 6,
            bytes_accessed=rows * width * 4 + width * FF * 6,
            transcendentals=rows * FF,
        ),
        name="run_expert",
    )(arrived, w_gu, w_down, produced)


def combine_kernel(x_ref, rank_ref, gate_ref, cotangent_ref, out_ref, grad_ref, sum_ref):
    step = pl.program_id(0)
    tokens, width = cotangent_ref.shape
    half = width // 2

    @pl.when(step == 0)
    def _():
        sum_ref[...] = jnp.zeros_like(sum_ref)

    rank = rank_ref[...][:, None, :]
    gate = gate_ref[...][:, None, :]
    shape = (GROUP, 8, tokens)
    row = lax.broadcasted_iota(jnp.int32, shape, 1)
    low = row < 4
    pieces = [
        (rank == row, 0, 0, width),
        (rank == row + 8, width, 0, width),
        ((rank == row + 16) & low, 2 * width, 0, half),
        ((rank == row + 12) & ~low, 2 * width, half, half),
    ]
    grad = jnp.zeros((GROUP, tokens), jnp.float32)
    for mask, source, place, count in pieces:
        rows = in_rows(x_ref[:, :, source : source + count])
        weight = jnp.where(mask, gate, 0.0).reshape(-1, tokens).astype(jnp.bfloat16)
        sum_ref[:, place : place + count] += lax.dot_general(
            weight, rows, (((0,), (0,)), ((), ())), preferred_element_type=jnp.float32
        )
        inner = lax.dot_general(
            rows,
            cotangent_ref[:, place : place + count],
            (((1,), (1,)), ((), ())),
            preferred_element_type=jnp.float32,
        )
        grad += jnp.sum(jnp.where(mask, inner.reshape(shape), 0.0), axis=1)
    grad_ref[...] = grad

    @pl.when(step == pl.num_programs(0) - 1)
    def _():
        out_ref[...] = sum_ref[...].astype(jnp.bfloat16)


def combine(returned, rank, gate_of, cotangent):
    peers, _, packed = returned.shape
    tokens, width = cotangent.shape
    return pl.pallas_call(
        combine_kernel,
        grid=(peers // GROUP,),
        in_specs=[
            pl.BlockSpec((GROUP, 8, packed), lambda i: (i, 0, 0)),
            pl.BlockSpec((GROUP, tokens), lambda i: (i, 0)),
            pl.BlockSpec((GROUP, tokens), lambda i: (i, 0)),
            pl.BlockSpec((tokens, width), lambda i: (0, 0)),
        ],
        out_specs=[
            pl.BlockSpec((tokens, width), lambda i: (0, 0)),
            pl.BlockSpec((GROUP, tokens), lambda i: (i, 0)),
        ],
        out_shape=[
            jax.ShapeDtypeStruct((tokens, width), jnp.bfloat16),
            jax.ShapeDtypeStruct((peers, tokens), jnp.float32),
        ],
        scratch_shapes=[pltpu.VMEM((tokens, width), jnp.float32)],
        compiler_params=pltpu.CompilerParams(vmem_limit_bytes=40 * 1024 * 1024),
        cost_estimate=pl.CostEstimate(
            flops=peers * 24 * tokens * width * 4,
            bytes_accessed=peers * 40 * width + tokens * width * 4,
            transcendentals=0,
        ),
        name="combine",
    )(returned, rank, gate_of, cotangent)


def shards(
    tokens, cotangent, routes, gates, previous_row, gu_payload, gu_scales, down_payload, down_scales
):
    local_count, model_width = tokens.shape
    half = model_width // 2
    devices = lax.axis_size("expert")
    experts = previous_row.shape[0]
    device_id = lax.axis_index("expert")
    chip, core = device_id // 2, device_id % 2
    parity = core.astype(jnp.int32).reshape(1)
    same_core = [[2 * c + p for c in range(experts)] for p in range(2)]
    swap = [(d, d ^ 1) for d in range(devices)]

    def exchange(x):
        return lax.all_to_all(x, "expert", 0, 0, axis_index_groups=same_core, tiled=True)

    down_own = exchange(down_payload)
    packed = jnp.concatenate(
        [lax.dynamic_slice_in_dim(gu_payload, 4 * core + 8 * g, 8, axis=1) for g in range(3)]
        + [
            jnp.concatenate(
                [
                    lax.dynamic_slice_in_dim(gu_payload[:, :, half_ff : half_ff + FF], 24 - 24 * core, 4, axis=1)
                    for half_ff in (0, FF)
                ],
                axis=1,
            )
        ],
        axis=2,
    )
    gu_scale = jnp.repeat(gu_scales[chip], 128, axis=1)
    down_scale = jnp.repeat(down_scales[chip], 128, axis=1)

    routes_t = routes.T
    gates_t = gates.T.astype(jnp.float32)
    slots = jnp.arange(experts, dtype=jnp.int32)[None, :, None]
    target = jnp.sum(
        jnp.where(routes_t[:, None, :] == slots, previous_row[None, :, None], 0), axis=1
    )
    named = target[:, None, :] == slots
    member = jnp.any(named, axis=0)
    gate_of = jnp.sum(jnp.where(named, gates_t[:, None, :], 0.0), axis=0)
    earlier = jnp.arange(local_count)[:, None] < jnp.arange(local_count)[None, :]
    rank = jnp.dot(
        member.astype(jnp.bfloat16), earlier.astype(jnp.bfloat16), preferred_element_type=jnp.float32
    ).astype(jnp.int32)
    rank = jnp.where(member, rank, -1)

    def picked(places):
        select = (rank[:, None, :] == places[None, :, None]).astype(jnp.bfloat16)
        rows = jnp.dot(
            select.reshape(-1, local_count), tokens, preferred_element_type=jnp.float32
        ).astype(jnp.bfloat16)
        return rows.reshape(experts, places.shape[0], model_width)

    eight = jnp.arange(8, dtype=jnp.int32)
    outgoing_a = picked(eight)
    last = picked(16 + eight % 4)
    last = jnp.where(eight[None, :, None] < 4, last[:, :, :half], last[:, :, half:])
    outgoing_b = jnp.concatenate([picked(8 + eight), last], axis=2)

    packed, outgoing_a, outgoing_b, down_own, rank, gate_of, gu_scale, down_scale = (
        lax.optimization_barrier(
            (packed, outgoing_a, outgoing_b, down_own, rank, gate_of, gu_scale, down_scale)
        )
    )
    gu_own = exchange(packed)
    gu_own, outgoing_b = lax.optimization_barrier((gu_own, outgoing_b))
    gu_other = lax.ppermute(gu_own, "expert", swap)
    arrived_b = exchange(outgoing_b)
    arrived_b, gu_other, down_own, outgoing_a = lax.optimization_barrier(
        (arrived_b, gu_other, down_own, outgoing_a)
    )
    arrived_a = exchange(outgoing_a)
    down_other = lax.ppermute(down_own, "expert", swap)
    produced, w_gu, w_down = run_first(
        arrived_b, gu_own, gu_other, down_own, down_other, gu_scale, down_scale, parity, model_width
    )
    produced, arrived_a = lax.optimization_barrier((produced, arrived_a))
    produced = run_expert(arrived_a, w_gu, w_down, produced)
    returned = exchange(produced)
    layer_out, grad = combine(returned, rank, gate_of, cotangent)
    gate_grad = jnp.sum(jnp.where(named, grad[None], 0.0), axis=1).T
    return (layer_out, gate_grad)


def solution(mesh):
    in_specs = (
        P("expert", None),
        P("expert", None),
        P("expert", None),
        P("expert", None),
        P(),
        P(None, "expert", None),
        P(),
        P(None, "expert", None),
        P(),
    )
    out_specs = (P("expert", None), P("expert", None))
    return jax.shard_map(shards, mesh=mesh, in_specs=in_specs, out_specs=out_specs, check_vma=False)
```

```python
import functools

import jax
import jax.numpy as jnp
from jax import lax
from jax.experimental import pallas as pl
from jax.experimental.pallas import tpu as pltpu
from jax.sharding import PartitionSpec as P

FF = 1024
TOP = 8
COLS = 256
GROUP = 16


def in_rows(block):
    return block.astype(jnp.float32).reshape(-1, block.shape[-1]).astype(jnp.bfloat16)


def restore(zero_gu, one_gu, zero_down, one_down, gu_scale_ref, down_scale_ref, step, gu_ref, down_ref):
    width = gu_ref.shape[1]
    chips = zero_gu.shape[0]
    tiles = []
    for chip in range(chips):
        zero = [zero_gu[chip, :, g * width : (g + 1) * width] for g in range(3)]
        one = [one_gu[chip, :, g * width : (g + 1) * width] for g in range(3)]
        fold_zero = zero_gu[chip, :, 3 * width :].astype(jnp.float32)
        fold_one = one_gu[chip, :, 3 * width :].astype(jnp.float32)
        middle = jnp.concatenate(
            [
                jnp.concatenate([fold_zero[:4], fold_one[:4]], axis=0),
                jnp.concatenate([fold_zero[4:], fold_one[4:]], axis=0),
            ],
            axis=1,
        )
        tiles += zero + [middle] + one
    for pair in range(len(tiles) // 2):
        scaled = []
        for k in (2 * pair, 2 * pair + 1):
            at = (step * 8 * len(tiles) + 8 * k) // 128
            scaled.append(tiles[k].astype(jnp.float32) * gu_scale_ref[pl.ds(at, 1), :])
        start = pl.multiple_of(step * 8 * len(tiles) + 16 * pair, 16)
        gu_ref[pl.ds(start, 16), :] = jnp.concatenate(scaled, axis=0).astype(jnp.bfloat16)
    scale = down_scale_ref[pl.ds(step * chips * 16 // 128, 1), :]
    for chip in range(chips):
        both = [ref[chip].astype(jnp.float32) * scale for ref in (zero_down, one_down)]
        start = pl.multiple_of((step * chips + chip) * 16, 16)
        down_ref[pl.ds(start, 16), :] = jnp.concatenate(both, axis=0).astype(jnp.bfloat16)


def expert_rows(place, parts, out_ref, gu_ref, down_ref, rows_ref, active_ref, ready):
    peers = parts[0].shape[0]
    width = rows_ref.shape[1]
    half = width // 2
    full, folded = len(parts) // 2, len(parts) % 2 == 1
    eight = 8 * peers
    chunks = FF // COLS

    for q in range(0, peers, 4):
        for g in range(2 * full):
            rows_ref[pl.ds(g // 2 * eight + 8 * q, 32), pl.ds(g % 2 * half, half)] = in_rows(
                parts[g][q : q + 4]
            )
        if folded:
            fold = [parts[-1][p].astype(jnp.float32) for p in range(q, q + 4)]
            for part, first in ((0, 0), (1, 4)):
                rows_ref[pl.ds(full * eight + 4 * q, 16), pl.ds(part * half, half)] = (
                    jnp.concatenate([f[first : first + 4] for f in fold], axis=0)
                ).astype(jnp.bfloat16)

    for j in range(chunks):
        ready(j)
        gate = jnp.dot(
            rows_ref[...], gu_ref[:, j * COLS : (j + 1) * COLS], preferred_element_type=jnp.float32
        )
        up = jnp.dot(
            rows_ref[...],
            gu_ref[:, FF + j * COLS : FF + (j + 1) * COLS],
            preferred_element_type=jnp.float32,
        )
        active_ref[:, j * COLS : (j + 1) * COLS] = (gate / (1.0 + jnp.exp(-gate)) * up).astype(
            jnp.bfloat16
        )
    ready(chunks)

    for j in range(half // COLS):
        sides = []
        for side in range(2):
            at = side * half + j * COLS
            y = jnp.dot(
                active_ref[...], down_ref[:, at : at + COLS], preferred_element_type=jnp.float32
            )
            sides.append(y)
            for g in range(full):
                to = place + g * width + at
                out_ref[:, :, to : to + COLS] = (
                    y[g * eight : (g + 1) * eight].reshape(peers, 8, COLS).astype(jnp.bfloat16)
                )
        if folded:
            for p in range(peers):
                at = full * eight + 4 * p
                to = place + full * width + j * COLS
                out_ref[p, :, to : to + COLS] = (
                    jnp.concatenate([sides[0][at : at + 4], sides[1][at : at + 4]], axis=0)
                ).astype(jnp.bfloat16)


def first_kernel(place, parity_ref, own_gu, other_gu, own_down, other_down, gu_scale_ref, down_scale_ref, x_a, x_b, x_c, out_ref, gu_hbm, down_hbm, gu_ref, down_ref, rows_ref, active_ref, sems):
    step = pl.program_id(0)
    restoring = gu_ref.shape[0] // (56 * own_gu.shape[0])
    scales = (gu_scale_ref, down_scale_ref)

    @pl.when((step < restoring) & (parity_ref[0] == 0))
    def _():
        restore(own_gu, other_gu, own_down, other_down, *scales, step, gu_ref, down_ref)

    @pl.when((step < restoring) & (parity_ref[0] != 0))
    def _():
        restore(other_gu, own_gu, other_down, own_down, *scales, step, gu_ref, down_ref)

    leaving = [
        pltpu.make_async_copy(gu_ref, gu_hbm, sems.at[0]),
        pltpu.make_async_copy(down_ref, down_hbm, sems.at[1]),
    ]

    @pl.when(step == restoring)
    def _():
        for copy in leaving:
            copy.start()

    @pl.when(step >= restoring)
    def _():
        expert_rows(
            place, (x_a, x_b, x_c), out_ref, gu_ref, down_ref, rows_ref, active_ref, lambda j: None
        )

    @pl.when(step == pl.num_programs(0) - 1)
    def _():
        for copy in leaving:
            copy.wait()


def run_first(own, other_gu, own_down, other_down, gu_scale, down_scale, parity, place):
    peers, _, packed = other_gu.shape
    width = down_scale.shape[1]
    each = 12
    total = width * 5 // 2
    group, chips = 32, 4
    restoring = peers // chips
    rows = peers * each

    def part(count):
        return pl.BlockSpec((chips, 8, count), lambda i: (jnp.minimum(i, restoring - 1), 0, 0))

    def piece(count, at=0):
        return pl.BlockSpec((group, 8, count), lambda i: (jnp.maximum(i - restoring, 0), 0, at))

    after = 2 * packed // width

    gu_shape, down_shape = (width, 2 * FF), (FF, width)
    return pl.pallas_call(
        functools.partial(first_kernel, place),
        grid=(restoring + peers // group,),
        in_specs=[
            pl.BlockSpec(memory_space=pltpu.SMEM),
            part(packed),
            part(packed),
            part(width),
            part(width),
            pl.BlockSpec(gu_scale.shape, lambda i: (0, 0)),
            pl.BlockSpec(down_scale.shape, lambda i: (0, 0)),
        ]
        + [piece(width // 2, after + k) for k in range(3)],
        out_specs=[piece(total), pl.BlockSpec(memory_space=pl.ANY), pl.BlockSpec(memory_space=pl.ANY)],
        out_shape=[
            jax.ShapeDtypeStruct((peers, 8, total), jnp.bfloat16),
            jax.ShapeDtypeStruct(gu_shape, jnp.bfloat16),
            jax.ShapeDtypeStruct(down_shape, jnp.bfloat16),
        ],
        scratch_shapes=[
            pltpu.VMEM(gu_shape, jnp.bfloat16),
            pltpu.VMEM(down_shape, jnp.bfloat16),
            pltpu.VMEM((group * each, width), jnp.bfloat16),
            pltpu.VMEM((group * each, FF), jnp.bfloat16),
            pltpu.SemaphoreType.DMA((2,)),
        ],
        compiler_params=pltpu.CompilerParams(vmem_limit_bytes=56 * 1024 * 1024),
        cost_estimate=pl.CostEstimate(
            flops=rows * width * FF * 6,
            bytes_accessed=rows * width * 4 + width * FF * 12,
            transcendentals=rows * FF,
        ),
        name="restore_and_run",
    )(parity, own, other_gu, own_down, other_down, gu_scale, down_scale, own, own, own)


def expert_kernel(x_a, x_b, gu_hbm, down_hbm, produced, out_ref, gu_ref, down_ref, rows_ref, active_ref, sems):
    step = pl.program_id(0)
    copies = []
    for j in range(FF // COLS):
        for start in (j * COLS, FF + j * COLS):
            part = (slice(None), pl.ds(start, COLS))
            copies.append(
                pltpu.make_async_copy(gu_hbm.at[part], gu_ref.at[part], sems.at[len(copies)])
            )
    copies.append(pltpu.make_async_copy(down_hbm, down_ref, sems.at[len(copies)]))

    @pl.when(step == 0)
    def _():
        for copy in copies:
            copy.start()

    def ready(j):
        @pl.when(step == 0)
        def _():
            for copy in copies[2 * j : 2 * j + 2]:
                copy.wait()

    expert_rows(0, (x_a, x_b), out_ref, gu_ref, down_ref, rows_ref, active_ref, ready)


def run_expert(arrived, w_gu, w_down, produced):
    peers, _, packed = arrived.shape
    width = w_gu.shape[0]
    each = 8 * packed // width
    group = 64
    rows = peers * each
    piece = pl.BlockSpec((group, 8, packed), lambda i: (i, 0, 0))
    halves = [pl.BlockSpec((group, 8, packed // 2), lambda i, at=at: (i, 0, at)) for at in range(2)]
    return pl.pallas_call(
        expert_kernel,
        grid=(peers // group,),
        in_specs=halves + [pl.BlockSpec(memory_space=pl.ANY)] * 3,
        out_specs=piece,
        out_shape=jax.ShapeDtypeStruct(produced.shape, jnp.bfloat16),
        input_output_aliases={4: 0},
        scratch_shapes=[
            pltpu.VMEM(w_gu.shape, jnp.bfloat16),
            pltpu.VMEM(w_down.shape, jnp.bfloat16),
            pltpu.VMEM((group * each, width), jnp.bfloat16),
            pltpu.VMEM((group * each, FF), jnp.bfloat16),
            pltpu.SemaphoreType.DMA((2 * FF // COLS + 1,)),
        ],
        compiler_params=pltpu.CompilerParams(vmem_limit_bytes=58 * 1024 * 1024),
        cost_estimate=pl.CostEstimate(
            flops=rows * width * FF * 6,
            bytes_accessed=rows * width * 4 + width * FF * 6,
            transcendentals=rows * FF,
        ),
        name="run_expert",
    )(arrived, arrived, w_gu, w_down, produced)


def combine_kernel(x_ref, rank_ref, gate_ref, cotangent_ref, out_ref, grad_ref, sum_ref):
    step = pl.program_id(0)
    tokens, width = cotangent_ref.shape
    half = width // 2

    @pl.when(step == 0)
    def _():
        sum_ref[...] = jnp.zeros_like(sum_ref)

    rank = rank_ref[...][:, None, :]
    gate = gate_ref[...][:, None, :]
    shape = (GROUP, 8, tokens)
    row = lax.broadcasted_iota(jnp.int32, shape, 1)
    low = row < 4
    pieces = [
        (rank == row, 0, 0, width),
        (rank == row + 8, width, 0, width),
        ((rank == row + 16) & low, 2 * width, 0, half),
        ((rank == row + 12) & ~low, 2 * width, half, half),
    ]
    grad = jnp.zeros((GROUP, tokens), jnp.float32)
    for mask, source, place, count in pieces:
        rows = in_rows(x_ref[:, :, source : source + count])
        weight = jnp.where(mask, gate, 0.0).reshape(-1, tokens).astype(jnp.bfloat16)
        sum_ref[:, place : place + count] += lax.dot_general(
            weight, rows, (((0,), (0,)), ((), ())), preferred_element_type=jnp.float32
        )
        inner = lax.dot_general(
            rows,
            cotangent_ref[:, place : place + count],
            (((1,), (1,)), ((), ())),
            preferred_element_type=jnp.float32,
        )
        grad += jnp.sum(jnp.where(mask, inner.reshape(shape), 0.0), axis=1)
    grad_ref[...] = grad

    @pl.when(step == pl.num_programs(0) - 1)
    def _():
        out_ref[...] = sum_ref[...].astype(jnp.bfloat16)


def combine(returned, rank, gate_of, cotangent):
    peers, _, packed = returned.shape
    tokens, width = cotangent.shape
    return pl.pallas_call(
        combine_kernel,
        grid=(peers // GROUP,),
        in_specs=[
            pl.BlockSpec((GROUP, 8, packed), lambda i: (i, 0, 0)),
            pl.BlockSpec((GROUP, tokens), lambda i: (i, 0)),
            pl.BlockSpec((GROUP, tokens), lambda i: (i, 0)),
            pl.BlockSpec((tokens, width), lambda i: (0, 0)),
        ],
        out_specs=[
            pl.BlockSpec((tokens, width), lambda i: (0, 0)),
            pl.BlockSpec((GROUP, tokens), lambda i: (i, 0)),
        ],
        out_shape=[
            jax.ShapeDtypeStruct((tokens, width), jnp.bfloat16),
            jax.ShapeDtypeStruct((peers, tokens), jnp.float32),
        ],
        scratch_shapes=[pltpu.VMEM((tokens, width), jnp.float32)],
        compiler_params=pltpu.CompilerParams(vmem_limit_bytes=40 * 1024 * 1024),
        cost_estimate=pl.CostEstimate(
            flops=peers * 24 * tokens * width * 4,
            bytes_accessed=peers * 40 * width + tokens * width * 4,
            transcendentals=0,
        ),
        name="combine",
    )(returned, rank, gate_of, cotangent)


def shards(
    tokens, cotangent, routes, gates, previous_row, gu_payload, gu_scales, down_payload, down_scales
):
    local_count, model_width = tokens.shape
    half = model_width // 2
    devices = lax.axis_size("expert")
    experts = previous_row.shape[0]
    device_id = lax.axis_index("expert")
    chip, core = device_id // 2, device_id % 2
    parity = core.astype(jnp.int32).reshape(1)
    same_core = [[2 * c + p for c in range(experts)] for p in range(2)]
    swap = [(d, d ^ 1) for d in range(devices)]

    def exchange(x):
        return lax.all_to_all(x, "expert", 0, 0, axis_index_groups=same_core, tiled=True)

    down_own = exchange(down_payload)
    gu_parts = [lax.dynamic_slice_in_dim(gu_payload, 4 * core + 8 * g, 8, axis=1) for g in range(3)]
    gu_fold = [
        lax.dynamic_slice_in_dim(gu_payload[:, :, at : at + FF], 24 - 24 * core, 4, axis=1)
        for at in (0, FF)
    ]
    gu_parts.append(jnp.concatenate(gu_fold, axis=1))
    gu_scale = jnp.repeat(gu_scales[chip], 128, axis=1)
    down_scale = jnp.repeat(down_scales[chip], 128, axis=1)

    routes_t = routes.T
    gates_t = gates.T.astype(jnp.float32)
    slots = jnp.arange(experts, dtype=jnp.int32)[None, :, None]
    target = jnp.sum(
        jnp.where(routes_t[:, None, :] == slots, previous_row[None, :, None], 0), axis=1
    )
    named = target[:, None, :] == slots
    member = jnp.any(named, axis=0)
    gate_of = jnp.sum(jnp.where(named, gates_t[:, None, :], 0.0), axis=0)
    earlier = jnp.arange(local_count)[:, None] < jnp.arange(local_count)[None, :]
    rank = jnp.dot(
        member.astype(jnp.bfloat16), earlier.astype(jnp.bfloat16), preferred_element_type=jnp.float32
    ).astype(jnp.int32)
    rank = jnp.where(member, rank, -1)

    def picked(places):
        select = (rank[:, None, :] == places[None, :, None]).astype(jnp.bfloat16)
        rows = jnp.dot(
            select.reshape(-1, local_count), tokens, preferred_element_type=jnp.float32
        ).astype(jnp.bfloat16)
        return rows.reshape(experts, places.shape[0], model_width)

    eight = jnp.arange(8, dtype=jnp.int32)
    outgoing_a = picked(eight)
    last = picked(16 + eight % 4)
    last = jnp.where(eight[None, :, None] < 4, last[:, :, :half], last[:, :, half:])
    packed = jnp.concatenate(gu_parts + [picked(8 + eight), last], axis=2)
    gu_width = 7 * FF

    packed, outgoing_a, down_own, rank, gate_of, gu_scale, down_scale = lax.optimization_barrier(
        (packed, outgoing_a, down_own, rank, gate_of, gu_scale, down_scale)
    )
    own = exchange(packed)
    own, down_own, outgoing_a = lax.optimization_barrier((own, down_own, outgoing_a))
    arrived_a = exchange(outgoing_a)
    down_other = lax.ppermute(down_own, "expert", swap)
    gu_other = lax.ppermute(own[:, :, :gu_width], "expert", swap)
    produced, w_gu, w_down = run_first(
        own, gu_other, down_own, down_other, gu_scale, down_scale, parity, model_width
    )
    produced, arrived_a = lax.optimization_barrier((produced, arrived_a))
    produced = run_expert(arrived_a, w_gu, w_down, produced)
    returned = exchange(produced)
    layer_out, grad = combine(returned, rank, gate_of, cotangent)
    gate_grad = jnp.sum(jnp.where(named, grad[None], 0.0), axis=1).T
    return (layer_out, gate_grad)


def solution(mesh):
    in_specs = (
        P("expert", None),
        P("expert", None),
        P("expert", None),
        P("expert", None),
        P(),
        P(None, "expert", None),
        P(),
        P(None, "expert", None),
        P(),
    )
    out_specs = (P("expert", None), P("expert", None))
    return jax.shard_map(shards, mesh=mesh, in_specs=in_specs, out_specs=out_specs, check_vma=False)
```

```python
import functools

import jax
import jax.numpy as jnp
from jax import lax
from jax.experimental import pallas as pl
from jax.experimental.pallas import tpu as pltpu
from jax.sharding import PartitionSpec as P

FF = 1024
TOP = 8
COLS = 256
GROUP = 32


def in_rows(block):
    return block.astype(jnp.float32).reshape(-1, block.shape[-1]).astype(jnp.bfloat16)


def restore(zero_gu, one_gu, zero_down, one_down, gu_scale_ref, down_scale_ref, step, gu_ref, down_ref):
    width = gu_ref.shape[1]
    chips = zero_gu.shape[0]
    tiles = []
    for chip in range(chips):
        zero = [zero_gu[chip, :, g * width : (g + 1) * width] for g in range(3)]
        one = [one_gu[chip, :, g * width : (g + 1) * width] for g in range(3)]
        fold_zero = zero_gu[chip, :, 3 * width :].astype(jnp.float32)
        fold_one = one_gu[chip, :, 3 * width :].astype(jnp.float32)
        middle = jnp.concatenate(
            [
                jnp.concatenate([fold_zero[:4], fold_one[:4]], axis=0),
                jnp.concatenate([fold_zero[4:], fold_one[4:]], axis=0),
            ],
            axis=1,
        )
        tiles += zero + [middle] + one
    for pair in range(len(tiles) // 2):
        scaled = []
        for k in (2 * pair, 2 * pair + 1):
            at = (step * 8 * len(tiles) + 8 * k) // 128
            scaled.append(tiles[k].astype(jnp.float32) * gu_scale_ref[pl.ds(at, 1), :])
        start = pl.multiple_of(step * 8 * len(tiles) + 16 * pair, 16)
        gu_ref[pl.ds(start, 16), :] = jnp.concatenate(scaled, axis=0).astype(jnp.bfloat16)
    scale = down_scale_ref[pl.ds(step * chips * 16 // 128, 1), :]
    for chip in range(chips):
        both = [ref[chip].astype(jnp.float32) * scale for ref in (zero_down, one_down)]
        start = pl.multiple_of((step * chips + chip) * 16, 16)
        down_ref[pl.ds(start, 16), :] = jnp.concatenate(both, axis=0).astype(jnp.bfloat16)


def expert_rows(place, parts, out_ref, gu_ref, down_ref, rows_ref, active_ref, ready):
    peers = parts[0].shape[0]
    width = rows_ref.shape[1]
    half = width // 2
    full, folded = len(parts) // 2, len(parts) % 2 == 1
    eight = 8 * peers
    chunks = FF // COLS

    for q in range(0, peers, 4):
        for g in range(2 * full):
            rows_ref[pl.ds(g // 2 * eight + 8 * q, 32), pl.ds(g % 2 * half, half)] = in_rows(
                parts[g][q : q + 4]
            )
        if folded:
            fold = [parts[-1][p].astype(jnp.float32) for p in range(q, q + 4)]
            for part, first in ((0, 0), (1, 4)):
                rows_ref[pl.ds(full * eight + 4 * q, 16), pl.ds(part * half, half)] = (
                    jnp.concatenate([f[first : first + 4] for f in fold], axis=0)
                ).astype(jnp.bfloat16)

    for j in range(chunks):
        ready(j)
        gate = jnp.dot(
            rows_ref[...], gu_ref[:, j * COLS : (j + 1) * COLS], preferred_element_type=jnp.float32
        )
        up = jnp.dot(
            rows_ref[...],
            gu_ref[:, FF + j * COLS : FF + (j + 1) * COLS],
            preferred_element_type=jnp.float32,
        )
        active_ref[:, j * COLS : (j + 1) * COLS] = (gate / (1.0 + jnp.exp(-gate)) * up).astype(
            jnp.bfloat16
        )
    ready(chunks)

    for j in range(half // COLS):
        sides = []
        for side in range(2):
            at = side * half + j * COLS
            y = jnp.dot(
                active_ref[...], down_ref[:, at : at + COLS], preferred_element_type=jnp.float32
            )
            sides.append(y)
            for g in range(full):
                to = place + g * width + at
                out_ref[:, :, to : to + COLS] = (
                    y[g * eight : (g + 1) * eight].reshape(peers, 8, COLS).astype(jnp.bfloat16)
                )
        if folded:
            for p in range(peers):
                at = full * eight + 4 * p
                to = place + full * width + j * COLS
                out_ref[p, :, to : to + COLS] = (
                    jnp.concatenate([sides[0][at : at + 4], sides[1][at : at + 4]], axis=0)
                ).astype(jnp.bfloat16)


def first_kernel(place, parity_ref, own_gu, other_gu, own_down, other_down, gu_scale_ref, down_scale_ref, x_a, x_b, x_c, out_ref, gu_hbm, down_hbm, gu_ref, down_ref, rows_ref, active_ref, sems):
    step = pl.program_id(0)
    restoring = gu_ref.shape[0] // (56 * own_gu.shape[0])
    scales = (gu_scale_ref, down_scale_ref)

    @pl.when((step < restoring) & (parity_ref[0] == 0))
    def _():
        restore(own_gu, other_gu, own_down, other_down, *scales, step, gu_ref, down_ref)

    @pl.when((step < restoring) & (parity_ref[0] != 0))
    def _():
        restore(other_gu, own_gu, other_down, own_down, *scales, step, gu_ref, down_ref)

    leaving = [
        pltpu.make_async_copy(gu_ref, gu_hbm, sems.at[0]),
        pltpu.make_async_copy(down_ref, down_hbm, sems.at[1]),
    ]

    @pl.when(step == restoring)
    def _():
        for copy in leaving:
            copy.start()

    @pl.when(step >= restoring)
    def _():
        expert_rows(
            place, (x_a, x_b, x_c), out_ref, gu_ref, down_ref, rows_ref, active_ref, lambda j: None
        )

    @pl.when(step == pl.num_programs(0) - 1)
    def _():
        for copy in leaving:
            copy.wait()


def run_first(own, other_gu, own_down, other_down, gu_scale, down_scale, parity, place):
    peers, _, packed = other_gu.shape
    width = down_scale.shape[1]
    each = 12
    total = width * 5 // 2
    group, chips = 32, 4
    restoring = peers // chips
    rows = peers * each

    def part(count):
        return pl.BlockSpec((chips, 8, count), lambda i: (jnp.minimum(i, restoring - 1), 0, 0))

    def piece(count, at=0):
        return pl.BlockSpec((group, 8, count), lambda i: (jnp.maximum(i - restoring, 0), 0, at))

    after = 2 * packed // width

    gu_shape, down_shape = (width, 2 * FF), (FF, width)
    return pl.pallas_call(
        functools.partial(first_kernel, place),
        grid=(restoring + peers // group,),
        in_specs=[
            pl.BlockSpec(memory_space=pltpu.SMEM),
            part(packed),
            part(packed),
            part(width),
            part(width),
            pl.BlockSpec(gu_scale.shape, lambda i: (0, 0)),
            pl.BlockSpec(down_scale.shape, lambda i: (0, 0)),
        ]
        + [piece(width // 2, after + k) for k in range(3)],
        out_specs=[piece(total), pl.BlockSpec(memory_space=pl.ANY), pl.BlockSpec(memory_space=pl.ANY)],
        out_shape=[
            jax.ShapeDtypeStruct((peers, 8, total), jnp.bfloat16),
            jax.ShapeDtypeStruct(gu_shape, jnp.bfloat16),
            jax.ShapeDtypeStruct(down_shape, jnp.bfloat16),
        ],
        scratch_shapes=[
            pltpu.VMEM(gu_shape, jnp.bfloat16),
            pltpu.VMEM(down_shape, jnp.bfloat16),
            pltpu.VMEM((group * each, width), jnp.bfloat16),
            pltpu.VMEM((group * each, FF), jnp.bfloat16),
            pltpu.SemaphoreType.DMA((2,)),
        ],
        compiler_params=pltpu.CompilerParams(vmem_limit_bytes=56 * 1024 * 1024),
        cost_estimate=pl.CostEstimate(
            flops=rows * width * FF * 6,
            bytes_accessed=rows * width * 4 + width * FF * 12,
            transcendentals=rows * FF,
        ),
        name="restore_and_run",
    )(parity, own, other_gu, own_down, other_down, gu_scale, down_scale, own, own, own)


def expert_kernel(x_a, x_b, gu_hbm, down_hbm, produced, out_ref, gu_ref, down_ref, rows_ref, active_ref, sems):
    step = pl.program_id(0)
    copies = []
    for j in range(FF // COLS):
        for start in (j * COLS, FF + j * COLS):
            part = (slice(None), pl.ds(start, COLS))
            copies.append(
                pltpu.make_async_copy(gu_hbm.at[part], gu_ref.at[part], sems.at[len(copies)])
            )
    copies.append(pltpu.make_async_copy(down_hbm, down_ref, sems.at[len(copies)]))

    @pl.when(step == 0)
    def _():
        for copy in copies:
            copy.start()

    def ready(j):
        @pl.when(step == 0)
        def _():
            for copy in copies[2 * j : 2 * j + 2]:
                copy.wait()

    expert_rows(0, (x_a, x_b), out_ref, gu_ref, down_ref, rows_ref, active_ref, ready)


def run_expert(arrived, w_gu, w_down, produced):
    peers, _, packed = arrived.shape
    width = w_gu.shape[0]
    each = 8 * packed // width
    group = 64
    rows = peers * each
    piece = pl.BlockSpec((group, 8, packed), lambda i: (i, 0, 0))
    halves = [pl.BlockSpec((group, 8, packed // 2), lambda i, at=at: (i, 0, at)) for at in range(2)]
    return pl.pallas_call(
        expert_kernel,
        grid=(peers // group,),
        in_specs=halves + [pl.BlockSpec(memory_space=pl.ANY)] * 3,
        out_specs=piece,
        out_shape=jax.ShapeDtypeStruct(produced.shape, jnp.bfloat16),
        input_output_aliases={4: 0},
        scratch_shapes=[
            pltpu.VMEM(w_gu.shape, jnp.bfloat16),
            pltpu.VMEM(w_down.shape, jnp.bfloat16),
            pltpu.VMEM((group * each, width), jnp.bfloat16),
            pltpu.VMEM((group * each, FF), jnp.bfloat16),
            pltpu.SemaphoreType.DMA((2 * FF // COLS + 1,)),
        ],
        compiler_params=pltpu.CompilerParams(vmem_limit_bytes=58 * 1024 * 1024),
        cost_estimate=pl.CostEstimate(
            flops=rows * width * FF * 6,
            bytes_accessed=rows * width * 4 + width * FF * 6,
            transcendentals=rows * FF,
        ),
        name="run_expert",
    )(arrived, arrived, w_gu, w_down, produced)


def combine_kernel(x_ref, rank_ref, gate_ref, cotangent_ref, out_ref, grad_ref, sum_ref):
    step = pl.program_id(0)
    tokens, width = cotangent_ref.shape
    half = width // 2

    @pl.when(step == 0)
    def _():
        sum_ref[...] = jnp.zeros_like(sum_ref)

    rank = rank_ref[...][:, None, :]
    gate = gate_ref[...][:, None, :]
    shape = (GROUP, 8, tokens)
    row = lax.broadcasted_iota(jnp.int32, shape, 1)
    low = row < 4
    pieces = [
        (rank == row, 0, 0, width),
        (rank == row + 8, width, 0, width),
        ((rank == row + 16) & low, 2 * width, 0, half),
        ((rank == row + 12) & ~low, 2 * width, half, half),
    ]
    grad = jnp.zeros((GROUP, tokens), jnp.float32)
    for mask, source, place, count in pieces:
        rows = in_rows(x_ref[:, :, source : source + count])
        weight = jnp.where(mask, gate, 0.0).reshape(-1, tokens).astype(jnp.bfloat16)
        sum_ref[:, place : place + count] += lax.dot_general(
            weight, rows, (((0,), (0,)), ((), ())), preferred_element_type=jnp.float32
        )
        inner = lax.dot_general(
            rows,
            cotangent_ref[:, place : place + count],
            (((1,), (1,)), ((), ())),
            preferred_element_type=jnp.float32,
        )
        grad += jnp.sum(jnp.where(mask, inner.reshape(shape), 0.0), axis=1)
    grad_ref[...] = grad

    @pl.when(step == pl.num_programs(0) - 1)
    def _():
        out_ref[...] = sum_ref[...].astype(jnp.bfloat16)


def combine(returned, rank, gate_of, cotangent):
    peers, _, packed = returned.shape
    tokens, width = cotangent.shape
    return pl.pallas_call(
        combine_kernel,
        grid=(peers // GROUP,),
        in_specs=[
            pl.BlockSpec((GROUP, 8, packed), lambda i: (i, 0, 0)),
            pl.BlockSpec((GROUP, tokens), lambda i: (i, 0)),
            pl.BlockSpec((GROUP, tokens), lambda i: (i, 0)),
            pl.BlockSpec((tokens, width), lambda i: (0, 0)),
        ],
        out_specs=[
            pl.BlockSpec((tokens, width), lambda i: (0, 0)),
            pl.BlockSpec((GROUP, tokens), lambda i: (i, 0)),
        ],
        out_shape=[
            jax.ShapeDtypeStruct((tokens, width), jnp.bfloat16),
            jax.ShapeDtypeStruct((peers, tokens), jnp.float32),
        ],
        scratch_shapes=[pltpu.VMEM((tokens, width), jnp.float32)],
        compiler_params=pltpu.CompilerParams(vmem_limit_bytes=40 * 1024 * 1024),
        cost_estimate=pl.CostEstimate(
            flops=peers * 24 * tokens * width * 4,
            bytes_accessed=peers * 40 * width + tokens * width * 4,
            transcendentals=0,
        ),
        name="combine",
    )(returned, rank, gate_of, cotangent)


def shards(
    tokens, cotangent, routes, gates, previous_row, gu_payload, gu_scales, down_payload, down_scales
):
    local_count, model_width = tokens.shape
    half = model_width // 2
    devices = lax.axis_size("expert")
    experts = previous_row.shape[0]
    device_id = lax.axis_index("expert")
    chip, core = device_id // 2, device_id % 2
    parity = core.astype(jnp.int32).reshape(1)
    same_core = [[2 * c + p for c in range(experts)] for p in range(2)]
    swap = [(d, d ^ 1) for d in range(devices)]

    def exchange(x):
        return lax.all_to_all(x, "expert", 0, 0, axis_index_groups=same_core, tiled=True)

    down_own = exchange(down_payload)
    gu_parts = [lax.dynamic_slice_in_dim(gu_payload, 4 * core + 8 * g, 8, axis=1) for g in range(3)]
    gu_fold = [
        lax.dynamic_slice_in_dim(gu_payload[:, :, at : at + FF], 24 - 24 * core, 4, axis=1)
        for at in (0, FF)
    ]
    gu_parts.append(jnp.concatenate(gu_fold, axis=1))
    gu_scale = jnp.repeat(gu_scales[chip], 128, axis=1)
    down_scale = jnp.repeat(down_scales[chip], 128, axis=1)

    routes_t = routes.T
    gates_t = gates.T.astype(jnp.float32)
    slots = jnp.arange(experts, dtype=jnp.int32)[None, :, None]
    target = jnp.sum(
        jnp.where(routes_t[:, None, :] == slots, previous_row[None, :, None], 0), axis=1
    )
    named = target[:, None, :] == slots
    member = jnp.any(named, axis=0)
    gate_of = jnp.sum(jnp.where(named, gates_t[:, None, :], 0.0), axis=0)
    earlier = jnp.arange(local_count)[:, None] < jnp.arange(local_count)[None, :]
    rank = jnp.dot(
        member.astype(jnp.bfloat16), earlier.astype(jnp.bfloat16), preferred_element_type=jnp.float32
    ).astype(jnp.int32)
    rank = jnp.where(member, rank, -1)

    def picked(places):
        select = (rank[:, None, :] == places[None, :, None]).astype(jnp.bfloat16)
        rows = jnp.dot(
            select.reshape(-1, local_count), tokens, preferred_element_type=jnp.float32
        ).astype(jnp.bfloat16)
        return rows.reshape(experts, places.shape[0], model_width)

    eight = jnp.arange(8, dtype=jnp.int32)
    outgoing_a = picked(eight)
    last = picked(16 + eight % 4)
    last = jnp.where(eight[None, :, None] < 4, last[:, :, :half], last[:, :, half:])
    packed = jnp.concatenate(gu_parts + [picked(8 + eight), last], axis=2)
    gu_width = 7 * FF

    packed, outgoing_a, down_own, rank, gate_of, gu_scale, down_scale = lax.optimization_barrier(
        (packed, outgoing_a, down_own, rank, gate_of, gu_scale, down_scale)
    )
    own = exchange(packed)
    own, down_own, outgoing_a = lax.optimization_barrier((own, down_own, outgoing_a))
    arrived_a = exchange(outgoing_a)
    down_other = lax.ppermute(down_own, "expert", swap)
    gu_other = lax.ppermute(own[:, :, :gu_width], "expert", swap)
    produced, w_gu, w_down = run_first(
        own, gu_other, down_own, down_other, gu_scale, down_scale, parity, model_width
    )
    produced, arrived_a = lax.optimization_barrier((produced, arrived_a))
    produced = run_expert(arrived_a, w_gu, w_down, produced)
    returned = exchange(produced)
    layer_out, grad = combine(returned, rank, gate_of, cotangent)
    gate_grad = jnp.sum(jnp.where(named, grad[None], 0.0), axis=1).T
    return (layer_out, gate_grad)


def solution(mesh):
    in_specs = (
        P("expert", None),
        P("expert", None),
        P("expert", None),
        P("expert", None),
        P(),
        P(None, "expert", None),
        P(),
        P(None, "expert", None),
        P(),
    )
    out_specs = (P("expert", None), P("expert", None))
    return jax.shard_map(shards, mesh=mesh, in_specs=in_specs, out_specs=out_specs, check_vma=False)
```
